512 devices in a mesh: dp: 4 (over y_hi, core), seq: 128 (over x, y_lo, z).
Axes of the slice: x: 4, y: 4 (y_hi: 2, y_lo: 2; y = y_hi * 2 + y_lo), z: 16, core: 2. Of those that a mesh axis runs over, the one named last changes fastest.
Arguments:
- clip_frames: bfloat16 [512, 16, 128, 128], P(('dp', 'seq')), parts along dimension 0, may hold values from -6 to 6
- cotangent: bfloat16 [512, 16, 128, 128], P(('dp', 'seq')), parts along dimension 0, may hold values from -6 to 6
- spatial_weight: bfloat16 [3, 3, 16, 16], replicated, may hold values from -0.5 to 0.5
- temporal_weight: bfloat16 [3, 3, 16, 16], replicated, may hold values from -0.4375 to 0.4375
Outputs:
- block_output: bfloat16 [512, 16, 128, 128], P(('dp', 'seq')), parts along dimension 0
- clip_grad: bfloat16 [512, 16, 128, 128], P(('dp', 'seq')), parts along dimension 0
- spatial_grad: float32 [12, 3, 16, 16], P('dp'), parts along dimension 0
- temporal_grad: float32 [12, 3, 16, 16], P('dp'), parts along dimension 0
The draws below stay inside these ranges and needn't reach their ends.
There are 4 independent parts, one for each index of `dp`. The reference program is written for one: setup_inputs(seed, part) draws one part's arguments, and reference() takes and returns one part's arrays. A program takes and returns all parts, laid end to end along the dimension named above; an argument that names none is the same for every part. Nothing has to cross between parts.
All inputs are finite; a program needn't handle non-finite values.
Results may differ from the reference program's by a relative error of at most 0.0071.
Values may be sent and summed in bfloat16 or wider, within the bound.
A program may use at most 64 MiB of HBM per device.

```python
import math
import jax
import jax.numpy as jnp
from jax import lax

C = 16
ROWS = 128
W = 128
LAYERS = 3
FRAMES = 128


def block_levels(rng, dims, shards, least, high):
    level, own = 1.0, jax.random.fold_in(rng, 6)
    for axis_at, parts in shards:
        heights = jnp.exp(jax.random.uniform(jax.random.fold_in(own, axis_at), (parts,), jnp.float32, least / len(shards), high / len(shards)))
        level = level * jnp.repeat(heights, dims[axis_at] // parts).reshape([-1 if axis == axis_at else 1 for axis in range(len(dims))])
    return level


def noise(key, dims, width, most, pieces=(), held_as=jnp.bfloat16):
    entries = width * jax.random.normal(key, dims, jnp.float32)
    if pieces:
        entries = entries * block_levels(key, dims, pieces, -0.22, 0.18)
    return jnp.clip(entries, -most, most).astype(held_as)


def setup_inputs(seed: int = 0, part: int = 0) -> dict:
    arg_keys = jax.random.split(jax.random.key(seed), 5)
    part_keys = jax.random.split(jax.random.fold_in(arg_keys[4], part), 5)
    return {
        "clip_frames": noise(part_keys[0], (FRAMES, C, ROWS, W), 1.0, 6.0, ((0, 128),)),
        "cotangent": noise(part_keys[1], (FRAMES, C, ROWS, W), 1.0, 6.0, ((0, 128),)),
        "spatial_weight": noise(arg_keys[2], (3, 3, C, C), (9 * C) ** -0.5, 0.5),
        "temporal_weight": noise(arg_keys[3], (LAYERS, 3, C, C), (12 * C) ** -0.5, 0.4375),
    }


def shifted(values, row_step, col_step):
    row_count = values.shape[2]
    col_count = values.shape[3]
    padded = jnp.pad(values, ((0, 0), (0, 0), (1, 1), (1, 1)))
    return padded[:, :, 1 + row_step:1 + row_step + row_count, 1 + col_step:1 + col_step + col_count]

def patches_of(values, orient):
    return jnp.concatenate([shifted(values, orient * (a - 1), orient * (b - 1)) for a in range(3) for b in range(3)], axis=1)

def time_shift(values, offset):
    length = values.shape[0]
    if abs(offset) >= length:
        return jnp.zeros_like(values)
    if offset > 0:
        return jnp.concatenate([values[offset:], jnp.zeros_like(values[:offset])], axis=0)
    if offset < 0:
        return jnp.concatenate([jnp.zeros_like(values[offset:]), values[:offset]], axis=0)
    return values

def silu_slope(preact):
    sigma = jax.nn.sigmoid(preact)
    return sigma * (1.0 + preact * (1.0 - sigma))

def reference(clip_frames, cotangent, spatial_weight, temporal_weight):
    flat_weight = spatial_weight.reshape(9 * C, C).astype(jnp.float32)
    mixing = spatial_weight.transpose(2, 0, 1, 3).reshape(C, 9 * C).astype(jnp.float32)
    frames = clip_frames.reshape(FRAMES, 1, C, ROWS, W)

    def forward_frame(single):
        return jnp.einsum('fkhw,kd->fdhw', patches_of(single, 1).astype(jnp.float32), flat_weight)
    preact = lax.map(forward_frame, frames).reshape(FRAMES, C, ROWS, W)
    states = [jax.nn.silu(preact).astype(jnp.bfloat16)]
    for layer in range(LAYERS):
        dilation = 2 ** layer
        current = states[-1]
        branch = current.astype(jnp.float32)
        for tap in range(3):
            branch = branch + jnp.einsum('tchw,cd->tdhw', time_shift(current, (tap - 1) * dilation).astype(jnp.float32), temporal_weight[layer, tap].astype(jnp.float32))
        states.append(branch.astype(jnp.bfloat16))
    block_output = states[-1]
    gradient = cotangent
    layer_terms = [None] * LAYERS
    for layer in reversed(range(LAYERS)):
        dilation = 2 ** layer
        current = states[layer]
        upper = gradient.astype(jnp.float32)
        layer_terms[layer] = jnp.stack([jnp.einsum('tchw,tdhw->cd', time_shift(current, (tap - 1) * dilation).astype(jnp.float32), upper) for tap in range(3)])
        total = upper
        for tap in range(3):
            total = total + jnp.einsum('tdhw,cd->tchw', time_shift(gradient, -(tap - 1) * dilation).astype(jnp.float32), temporal_weight[layer, tap].astype(jnp.float32))
        gradient = total.astype(jnp.bfloat16)
    slope = (gradient.astype(jnp.float32) * silu_slope(preact)).astype(jnp.bfloat16)

    def backward_frame(pair):
        single, grad_single = pair
        weight_term = jnp.einsum('fkhw,fdhw->kd', patches_of(single, 1).astype(jnp.float32), grad_single.astype(jnp.float32))
        input_term = jnp.einsum('fkhw,ck->fchw', patches_of(grad_single, -1).astype(jnp.float32), mixing)
        return (weight_term, input_term)
    weight_terms, input_terms = lax.map(backward_frame, (frames, slope.reshape(FRAMES, 1, C, ROWS, W)))
    factor = 1.0 / math.sqrt(FRAMES * ROWS * W)
    spatial_grad = lax.optimization_barrier(jnp.sum(weight_terms, axis=0)).reshape(3, 3, C, C) * factor
    clip_grad = input_terms.reshape(FRAMES, C, ROWS, W).astype(jnp.bfloat16)
    temporal_grad = jnp.stack(layer_terms) * factor
    return (block_output, clip_grad, spatial_grad, temporal_grad)
```

```python
import functools
import math

import jax
import jax.numpy as jnp
from jax import lax
from jax.experimental import pallas as pl
from jax.experimental.pallas import tpu as pltpu
from jax.sharding import PartitionSpec as P

MESH = pl.DeviceIdType.MESH
F32 = jnp.float32
BF16 = jnp.bfloat16
C = 16
N = 128
SEQ = 128
Z = 16
Q = SEQ // Z
G = 16
GROUPS = N // G
PAD = 4


def iota(shape, axis):
    return lax.broadcasted_iota(jnp.int32, shape, axis)


def mm(a, b):
    return lax.dot_general(a, b, (((1,), (0,)), ((), ())), preferred_element_type=F32)


def mm_nt(a, b):
    return lax.dot_general(a, b, (((1,), (1,)), ((), ())), preferred_element_type=F32)


def one_hot(cond):
    return jnp.where(cond, 1.0, 0.0).astype(BF16)


def banded(weights, span, offsets, transposed, out_channel_major=False):
    cols = span * C
    i = iota((G * C, cols), 0)
    j = iota((G * C, cols), 1)
    si = iota((G * C, C), 0)
    sj = iota((G * C, C), 1)
    if out_channel_major:
        place = i & (G - 1)
        spread = one_hot((si >> 4) == sj)
    else:
        place = i >> 4
        spread = one_hot((si & (C - 1)) == sj)
    tile = one_hot(iota((C, cols), 0) == (iota((C, cols), 1) & (C - 1)))
    diff = (j >> 4) - place
    total = jnp.zeros((G * C, cols), F32)
    for weight, offset in zip(weights, offsets):
        rows = (mm if transposed else mm_nt)(spread, weight).astype(BF16)
        total = jnp.where(diff == offset, mm(rows, tile), total)
    return total.astype(BF16)


def fold(acc, span, offset):
    rows = span * C
    diff = (iota((rows, G * C), 0) >> 4) - (iota((rows, G * C), 1) >> 4)
    kept = jnp.where(diff == offset, acc, 0.0)
    total = jnp.sum(kept.reshape(span, C, G * C), axis=0)
    total = total[:, :128] + total[:, 128:]
    for step in (64, 32, 16):
        total = total + pltpu.roll(total, step, 1)
    return total


def kernel(
    factor,
    clip_hbm, cot_hbm, sw_ref, tw_ref,
    out_hbm, grad_hbm, sgrad_ref, tgrad_ref,
    clip_in, cot_in, cot_f, act_f, xs, preact, bands_s, bands_v, bands_f, bands_b,
    back3, back2, back1, back0, st0, st1, st2, st3, grad_f, out_f, slopes,
    acc_t, acc_s, pack, sum1, part1, sum2, part2, sum3, out_v, grad_v,
    local_sem, send_sem, recv_sem,
):
    me = lax.axis_index("seq")
    q, z = me // Z, lax.rem(me, Z)

    cot_load = pltpu.make_async_copy(cot_hbm.at[0], cot_in, local_sem.at[0])
    cot_load.start()
    clip_load = pltpu.make_async_copy(clip_hbm.at[0], clip_in, local_sem.at[1])
    clip_load.start()

    barrier = pltpu.get_barrier_semaphore()

    @pl.loop(1, SEQ)
    def _(d):
        pl.semaphore_signal(barrier, inc=1, device_id={"seq": lax.rem(me + d, SEQ)}, device_id_type=MESH)

    def send_all(index, src, dst, at):
        def copy(k, j):
            t = lax.rem(q + k, Q) * Z + lax.rem(z + j, Z)
            return pltpu.make_async_remote_copy(
                src_ref=src.at[t], dst_ref=dst.at[at], send_sem=send_sem.at[index], recv_sem=recv_sem.at[index],
                device_id={"seq": t}, device_id_type=MESH,
            )

        @pl.loop(1, SEQ)
        def _(d):
            copy(d // Z, lax.rem(d, Z)).start()

    def wait_all(sem, ref):
        part = ref.at[pl.ds(0, SEQ - 1)]
        pltpu.make_async_copy(part, part, sem).wait()

    i = iota((G * C, G * C), 0)
    j = iota((G * C, G * C), 1)
    swap = one_hot(((i & (C - 1)) == (j >> 4)) & ((i >> 4) == (j & (G - 1))))

    cot_load.wait()

    @pl.loop(0, GROUPS)
    def _(g):
        rows = pl.ds(pl.multiple_of(g * G, G), G)
        cot_f[rows] = mm(swap, cot_in[:, rows, :].reshape(C * G, N)).astype(BF16).reshape(G, C, N)

    pl.semaphore_wait(barrier, SEQ - 1)
    send_all(0, cot_f, back3, me + PAD)
    back3[me + PAD] = cot_f[me]

    clip_load.wait()
    for b in range(3):
        bands_s[b] = banded([sw_ref[a, b] for a in range(3)], G + 2, range(3), False)
        xs[b, 0] = jnp.zeros((C, N), BF16)
        xs[b, N + 1] = jnp.zeros((C, N), BF16)
    lane = iota((G * C, N), 1)

    @pl.loop(0, GROUPS)
    def _(g):
        rows = pl.ds(pl.multiple_of(g * G, G), G)
        x = mm(swap, clip_in[:, rows, :].reshape(C * G, N))
        padded = pl.ds(g * G + 1, G)
        xs[0, padded] = jnp.where(lane == 0, 0.0, pltpu.roll(x, 1, 1)).astype(BF16).reshape(G, C, N)
        xs[1, padded] = x.astype(BF16).reshape(G, C, N)
        xs[2, padded] = jnp.where(lane == N - 1, 0.0, pltpu.roll(x, N - 1, 1)).astype(BF16).reshape(G, C, N)

    @pl.loop(0, GROUPS)
    def _(g):
        p = jnp.zeros((G * C, N), F32)
        for b in range(3):
            p = p + mm(bands_s[b], xs[b, pl.ds(g * G, G + 2)].reshape((G + 2) * C, N))
        rows = pl.ds(g * G, G)
        preact[rows] = p.reshape(G, C, N)
        act_f[rows] = (p / (1.0 + jnp.exp(-p))).astype(BF16).reshape(G, C, N)

    send_all(1, act_f, st0, me + PAD)
    st0[me + PAD] = act_f[me]

    zeros = jnp.zeros((PAD, C, N), BF16)
    for ref in (back3, back2, back1, st0, st1, st2):
        ref[pl.ds(0, PAD)] = zeros
        ref[pl.ds(N + PAD, PAD)] = zeros
    for layer in range(3):
        e = 2**layer
        span = G + 2 * e
        taps = [tw_ref[layer, k] for k in range(3)]
        bands_b[layer, :, pl.ds(0, span * C)] = banded(taps, span, [(2 - k) * e for k in range(3)], True)
        bands_f[layer, :, pl.ds(0, span * C)] = banded(taps, span, [k * e for k in range(3)], False)

    def temporal(src, dst, bands, layer, pad):
        e = 2**layer
        span = G + 2 * e

        @pl.loop(0, GROUPS)
        def _(g):
            own = src[pl.ds(g * G + PAD, G)].reshape(G * C, N).astype(F32)
            wide = src[pl.ds(g * G + PAD - e, span)].reshape(span * C, N)
            new = own + mm(bands[layer, :, pl.ds(0, span * C)], wide)
            dst[pl.ds(g * G + pad, G)] = new.astype(BF16).reshape(G, C, N)

    wait_all(recv_sem.at[0], back3)
    temporal(back3, back2, bands_b, 2, PAD)
    temporal(back2, back1, bands_b, 1, PAD)
    temporal(back1, back0, bands_b, 0, 0)
    send_all(2, back0, grad_f, me)
    grad_f[me] = back0[me]
    for b in range(3):
        bands_v[b] = banded([sw_ref[a, b] for a in range(3)], G + 2, [2 - a for a in range(3)], True, True)
        slopes[b, 0] = jnp.zeros((C, N), BF16)
        slopes[b, N + 1] = jnp.zeros((C, N), BF16)

    wait_all(recv_sem.at[1], st0)
    temporal(st0, st1, bands_f, 0, PAD)
    temporal(st1, st2, bands_f, 1, PAD)
    temporal(st2, st3, bands_f, 2, 0)
    send_all(3, st3, out_f, me)
    out_f[me] = st3[me]

    block = iota((C, 128), 1) >> 4
    last = jnp.zeros((C, 128), F32)
    packed = jnp.zeros((C, 128), F32)
    for layer, (state, back) in enumerate(((st0, back1), (st1, back2), (st2, back3))):
        e = 2**layer
        span = G + 2 * e
        acc_t[...] = jnp.zeros_like(acc_t)

        @pl.loop(0, GROUPS)
        def _(g):
            wide = state[pl.ds(g * G + PAD - e, span)].reshape(span * C, N)
            own = back[pl.ds(g * G + PAD, G)].reshape(G * C, N)
            acc_t[pl.ds(0, span * C)] += mm_nt(wide, own)

        for k in range(3):
            folded = fold(acc_t[pl.ds(0, span * C)], span, k * e)
            if layer * 3 + k < 8:
                packed = jnp.where(block == layer * 3 + k, folded, packed)
            else:
                last = jnp.where(block == 1, folded, last)
    pack[pl.ds(2, 2)] = packed.reshape(2, 8, 128)

    wait_all(recv_sem.at[2], grad_f)

    @pl.loop(0, GROUPS)
    def _(g):
        rows = pl.ds(g * G, G)
        p = preact[rows].reshape(G * C, N)
        s = 1.0 / (1.0 + jnp.exp(-p))
        slope = grad_f[rows].reshape(G * C, N).astype(F32) * (s * (1.0 + p * (1.0 - s)))
        padded = pl.ds(g * G + 1, G)
        slopes[0, padded] = jnp.where(lane == N - 1, 0.0, pltpu.roll(slope, N - 1, 1)).astype(BF16).reshape(G, C, N)
        slopes[1, padded] = slope.astype(BF16).reshape(G, C, N)
        slopes[2, padded] = jnp.where(lane == 0, 0.0, pltpu.roll(slope, 1, 1)).astype(BF16).reshape(G, C, N)

    acc_s[...] = jnp.zeros_like(acc_s)

    @pl.loop(0, GROUPS)
    def _(g):
        own = slopes[1, pl.ds(g * G + 1, G)].reshape(G * C, N)
        for b in range(3):
            acc_s[b] += mm_nt(xs[b, pl.ds(g * G, G + 2)].reshape((G + 2) * C, N), own)

    packed = jnp.zeros((C, 128), F32)
    for b in range(3):
        for a in range(3):
            folded = fold(acc_s[b], G + 2, a)
            if a * 3 + b < 8:
                packed = jnp.where(block == a * 3 + b, folded, packed)
            else:
                last = jnp.where(block == 0, folded, last)
    pack[pl.ds(0, 2)] = packed.reshape(2, 8, 128)
    pack[pl.ds(4, 2)] = last.reshape(2, 8, 128)
    pack[pl.ds(6, 2)] = jnp.zeros((2, 8, 128), F32)

    def to_columns(src_of, dst, index):
        for d in range(1, Q):
            other = lax.rem(q + d, Q)
            pltpu.make_async_remote_copy(
                src_ref=src_of(other), dst_ref=dst.at[q], send_sem=send_sem.at[index], recv_sem=recv_sem.at[index],
                device_id={"seq": other * Z + z}, device_id_type=MESH,
            ).start()

    def wait_some(sem, ref, count):
        part = ref.at[pl.ds(0, count)]
        pltpu.make_async_copy(part, part, sem).wait()

    to_columns(lambda other: pack.at[other], sum1, 4)
    sum1[q] = pack[q]

    def clip_gradient(g):
        total = jnp.zeros((C * G, N), F32)
        for b in range(3):
            total = total + mm(bands_v[b], slopes[b, pl.ds(g * G, G + 2)].reshape((G + 2) * C, N))
        grad_v[:, pl.ds(pl.multiple_of(g * G, G), G), :] = total.astype(BF16).reshape(C, G, N)

    wait_some(recv_sem.at[4], sum1, Q - 1)
    part1[...] = jnp.sum(sum1[...], axis=0)
    for d in range(1, Z):
        other = lax.rem(z + d, Z)
        pltpu.make_async_remote_copy(
            src_ref=part1, dst_ref=sum2.at[z], send_sem=send_sem.at[5], recv_sem=recv_sem.at[5],
            device_id={"seq": q * Z + other}, device_id_type=MESH,
        ).start()
    sum2[z] = part1[...]

    @pl.loop(0, GROUPS)
    def _(g):
        clip_gradient(g)

    grad_store = pltpu.make_async_copy(grad_v, grad_hbm.at[0], local_sem.at[0])
    grad_store.start()

    wait_some(recv_sem.at[5], sum2, Z - 1)
    part2[...] = jnp.sum(sum2[...], axis=0)
    to_columns(lambda other: part2, sum3, 6)
    sum3[q] = part2[...]
    wait_some(recv_sem.at[6], sum3, Q - 1)

    spatial = sum3[pl.ds(0, 2)].reshape(C, 128) * factor
    temporal_sum = sum3[pl.ds(2, 2)].reshape(C, 128) * factor
    last = sum3[pl.ds(4, 2)].reshape(C, 128) * factor
    for tap in range(9):
        at = (128 - tap * C) % 128
        from_s, at_s = (spatial, at) if tap < 8 else (last, 0)
        from_t, at_t = (temporal_sum, at) if tap < 8 else (last, 128 - C)
        sgrad_ref[tap // 3, tap % 3] = pltpu.roll(from_s, at_s, 1)[:, :C]
        tgrad_ref[tap // 3, tap % 3] = pltpu.roll(from_t, at_t, 1)[:, :C]

    wait_all(recv_sem.at[3], out_f)

    @pl.loop(0, GROUPS)
    def _(g):
        rows = pl.ds(pl.multiple_of(g * G, G), G)
        out_v[:, rows, :] = mm(swap, out_f[rows].reshape(G * C, N)).astype(BF16).reshape(C, G, N)

    out_store = pltpu.make_async_copy(out_v, out_hbm.at[0], local_sem.at[1])
    out_store.start()

    for index, ref in enumerate((cot_f, act_f, back0, st3)):
        wait_all(send_sem.at[index], ref)
    wait_some(send_sem.at[4], sum1, Q - 1)
    wait_some(send_sem.at[5], sum2, Z - 1)
    wait_some(send_sem.at[6], sum3, Q - 1)
    grad_store.wait()
    out_store.wait()


def body(clip_frames, cotangent, spatial_weight, temporal_weight):
    factor = 1.0 / math.sqrt(N * N * N)
    vmem = pl.BlockSpec(memory_space=pltpu.VMEM)
    anywhere = pl.BlockSpec(memory_space=pl.ANY)
    frame = pltpu.VMEM((N, C, N), BF16)
    padded = pltpu.VMEM((N + 2 * PAD, C, N), BF16)
    return pl.pallas_call(
        functools.partial(kernel, factor),
        out_shape=(
            jax.ShapeDtypeStruct((1, C, N, N), BF16),
            jax.ShapeDtypeStruct((1, C, N, N), BF16),
            jax.ShapeDtypeStruct((3, 3, C, C), F32),
            jax.ShapeDtypeStruct((3, 3, C, C), F32),
        ),
        in_specs=[anywhere, anywhere, vmem, vmem],
        out_specs=(anywhere, anywhere, vmem, vmem),
        scratch_shapes=[
            pltpu.VMEM((C, N, N), BF16),
            pltpu.VMEM((C, N, N), BF16),
            frame,
            frame,
            pltpu.VMEM((3, N + 2, C, N), BF16),
            pltpu.VMEM((N, C, N), F32),
            pltpu.VMEM((3, G * C, (G + 2) * C), BF16),
            pltpu.VMEM((3, G * C, (G + 2) * C), BF16),
            pltpu.VMEM((3, G * C, (G + 8) * C), BF16),
            pltpu.VMEM((3, G * C, (G + 8) * C), BF16),
            padded, padded, padded, frame,
            padded, padded, padded, frame,
            frame,
            frame,
            pltpu.VMEM((3, N + 2, C, N), BF16),
            pltpu.VMEM(((G + 8) * C, G * C), F32),
            pltpu.VMEM((3, (G + 2) * C, G * C), F32),
            pltpu.VMEM((Q, 8, 128), F32),
            pltpu.VMEM((Q, 8, 128), F32),
            pltpu.VMEM((8, 128), F32),
            pltpu.VMEM((Z, 8, 128), F32),
            pltpu.VMEM((8, 128), F32),
            pltpu.VMEM((Q, 8, 128), F32),
            pltpu.VMEM((C, N, N), BF16),
            pltpu.VMEM((C, N, N), BF16),
            pltpu.SemaphoreType.DMA((2,)),
            pltpu.SemaphoreType.DMA((7,)),
            pltpu.SemaphoreType.DMA((7,)),
        ],
        compiler_params=pltpu.CompilerParams(collective_id=0, has_side_effects=True, vmem_limit_bytes=40 << 20),
    )(clip_frames, cotangent, spatial_weight, temporal_weight)


def solution(mesh):
    placed = (P(("dp", "seq"), None, None, None), P(("dp", "seq"), None, None, None), P(), P())
    return jax.shard_map(
        body,
        mesh=mesh,
        in_specs=placed,
        out_specs=(
            P(("dp", "seq"), None, None, None),
            P(("dp", "seq"), None, None, None),
            P("dp", None, None, None),
            P("dp", None, None, None),
        ),
        check_vma=False,
    )
```

```python
import functools
import math

import jax
import jax.numpy as jnp
from jax import lax
from jax.experimental import pallas as pl
from jax.experimental.pallas import tpu as pltpu
from jax.sharding import PartitionSpec as P

MESH = pl.DeviceIdType.MESH
F32 = jnp.float32
BF16 = jnp.bfloat16
C = 16
N = 128
SEQ = 128
Z = 16
Q = SEQ // Z
G = 16
GROUPS = N // G
PAD = 4
PIECE = 5
VMEM_LIMIT = 60 << 20


def iota(shape, axis):
    return lax.broadcasted_iota(jnp.int32, shape, axis)


def mm(a, b):
    return lax.dot_general(a, b, (((1,), (0,)), ((), ())), preferred_element_type=F32)


def mm_nt(a, b):
    return lax.dot_general(a, b, (((1,), (1,)), ((), ())), preferred_element_type=F32)


def one_hot(cond):
    return jnp.where(cond, 1.0, 0.0).astype(BF16)


def banded(weights, span, offsets, transposed, out_channel_major=False):
    cols = span * C
    i = iota((G * C, cols), 0)
    j = iota((G * C, cols), 1)
    si = iota((G * C, C), 0)
    sj = iota((G * C, C), 1)
    if out_channel_major:
        place = i & (G - 1)
        spread = one_hot((si >> 4) == sj)
    else:
        place = i >> 4
        spread = one_hot((si & (C - 1)) == sj)
    tile = one_hot(iota((C, cols), 0) == (iota((C, cols), 1) & (C - 1)))
    diff = (j >> 4) - place
    total = jnp.zeros((G * C, cols), F32)
    for weight, offset in zip(weights, offsets):
        rows = (mm if transposed else mm_nt)(spread, weight).astype(BF16)
        total = jnp.where(diff == offset, mm(rows, tile), total)
    return total.astype(BF16)


def fold(acc, span, offset):
    rows = span * C
    diff = (iota((rows, G * C), 0) >> 4) - (iota((rows, G * C), 1) >> 4)
    kept = jnp.where(diff == offset, acc, 0.0)
    total = jnp.sum(kept.reshape(span, C, G * C), axis=0)
    total = total[:, :128] + total[:, 128:]
    for step in (64, 32, 16):
        total = total + pltpu.roll(total, step, 1)
    return total


def kernel(
    factor,
    clip_hbm, cot_hbm, sw_hbm, tw_hbm,
    out_hbm, grad_hbm, sgrad_ref, tgrad_ref,
    sw_ref, tw_ref, clip_in, cot_in, cot_f, act_f, xs, preact, bands_s, bands_v, bands_f, bands_b,
    back3, back2, back1, back0, st0, st1, st2, st3, grad_f, out_f, slopes,
    acc_t, acc_s, pack, sum1, part1, sum2, part2, sum3, total, out_v, grad_v,
    local_sem, send_sem, recv_sem, send_out, recv_grad, recv_out, ready,
):
    me = lax.axis_index("seq")
    q, z = me // Z, lax.rem(me, Z)

    cot_load = pltpu.make_async_copy(cot_hbm.at[0], cot_in, local_sem.at[0])
    cot_load.start()
    clip_load = pltpu.make_async_copy(clip_hbm.at[0], clip_in, local_sem.at[1])
    clip_load.start()
    sw_load = pltpu.make_async_copy(sw_hbm, sw_ref, local_sem.at[2])
    sw_load.start()
    tw_load = pltpu.make_async_copy(tw_hbm, tw_ref, local_sem.at[3])
    tw_load.start()

    barrier = pltpu.get_barrier_semaphore()
    for d in range(1, Q):
        pl.semaphore_signal(barrier, inc=1, device_id={"seq": lax.rem(q + d, Q) * Z + z}, device_id_type=MESH)
    for d in range(1, Z):
        pl.semaphore_signal(barrier, inc=1, device_id={"seq": q * Z + lax.rem(z + d, Z)}, device_id_type=MESH)

    def send_group(k, src, dst, at, sent, received):
        column = lax.rem(q + k, Q) * Z

        def send(i):
            j = 8 + lax.rem(i, 2) * (i + 1) // 2 - (1 - lax.rem(i, 2)) * (i // 2)
            t = column + lax.rem(z + j, Z)
            pltpu.make_async_remote_copy(
                src_ref=src.at[t], dst_ref=dst.at[at], send_sem=sent, recv_sem=received,
                device_id={"seq": t}, device_id_type=MESH,
            ).start()

        @pl.loop(0, Z if k else Z - 1)
        def _(i):
            send(i)

    def send_all(index, src, dst, at):
        for k in range(Q):
            send_group(k, src, dst, at, send_sem.at[index], recv_sem.at[index])

    def wait_some(sem, ref, count):
        part = ref.at[pl.ds(0, count)]
        pltpu.make_async_copy(part, part, sem).wait()

    def wait_all(sem, ref):
        wait_some(sem, ref, SEQ - 1)

    def wait_group(sem, ref, k):
        @pl.when(k == 0)
        def _():
            wait_some(sem, ref, Z - 1)

        @pl.when(k > 0)
        def _():
            wait_some(sem, ref, Z)

    i = iota((G * C, G * C), 0)
    j = iota((G * C, G * C), 1)
    swap = one_hot(((i & (C - 1)) == (j >> 4)) & ((i >> 4) == (j & (G - 1))))

    cot_load.wait()

    def cotangent_rows(k):
        rows = pl.ds(pl.multiple_of(lax.rem(q + k, Q) * G, G), G)
        cot_f[rows] = mm(swap, cot_in[:, rows, :].reshape(C * G, N)).astype(BF16).reshape(G, C, N)

    cotangent_rows(0)
    pl.semaphore_wait(barrier, Q - 1 + Z - 1)
    for d in range(1, Z):
        pl.semaphore_signal(ready, inc=1, device_id={"seq": q * Z + lax.rem(z + d, Z)}, device_id_type=MESH)
    send_group(0, cot_f, back3, me + PAD, send_sem.at[0], recv_sem.at[0])
    back3[me + PAD] = cot_f[me]

    @pl.loop(1, Q)
    def _(k):
        cotangent_rows(k)

    pl.semaphore_wait(ready, Z - 1)
    for k in range(1, Q):
        send_group(k, cot_f, back3, me + PAD, send_sem.at[0], recv_sem.at[0])

    clip_load.wait()
    sw_load.wait()
    tw_load.wait()
    for b in range(3):
        bands_s[b] = banded([sw_ref[a, b] for a in range(3)], G + 2, range(3), False)
        xs[b, 0] = jnp.zeros((C, N), BF16)
        xs[b, N + 1] = jnp.zeros((C, N), BF16)
    lane = iota((G * C, N), 1)

    @pl.loop(0, GROUPS)
    def _(g):
        rows = pl.ds(pl.multiple_of(g * G, G), G)
        x = mm(swap, clip_in[:, rows, :].reshape(C * G, N))
        padded = pl.ds(g * G + 1, G)
        xs[0, padded] = jnp.where(lane == 0, 0.0, pltpu.roll(x, 1, 1)).astype(BF16).reshape(G, C, N)
        xs[1, padded] = x.astype(BF16).reshape(G, C, N)
        xs[2, padded] = jnp.where(lane == N - 1, 0.0, pltpu.roll(x, N - 1, 1)).astype(BF16).reshape(G, C, N)

    @pl.loop(0, GROUPS)
    def _(g):
        p = jnp.zeros((G * C, N), F32)
        for b in range(3):
            p = p + mm(bands_s[b], xs[b, pl.ds(g * G, G + 2)].reshape((G + 2) * C, N))
        rows = pl.ds(g * G, G)
        preact[rows] = p.reshape(G, C, N)
        act_f[rows] = (p / (1.0 + jnp.exp(-p))).astype(BF16).reshape(G, C, N)

    send_all(1, act_f, st0, me + PAD)
    st0[me + PAD] = act_f[me]

    zeros = jnp.zeros((PAD, C, N), BF16)
    for ref in (back3, back2, back1, st0, st1, st2):
        ref[pl.ds(0, PAD)] = zeros
        ref[pl.ds(N + PAD, PAD)] = zeros
    for layer in range(3):
        e = 2**layer
        span = G + 2 * e
        taps = [tw_ref[layer, k] for k in range(3)]
        bands_b[layer, :, pl.ds(0, span * C)] = banded(taps, span, [(2 - k) * e for k in range(3)], True)
        bands_f[layer, :, pl.ds(0, span * C)] = banded(taps, span, [k * e for k in range(3)], False)

    def temporal(src, dst, bands, layer, pad):
        e = 2**layer
        span = G + 2 * e

        @pl.loop(0, GROUPS)
        def _(g):
            own = src[pl.ds(g * G + PAD, G)].reshape(G * C, N).astype(F32)
            wide = src[pl.ds(g * G + PAD - e, span)].reshape(span * C, N)
            new = own + mm(bands[layer, :, pl.ds(0, span * C)], wide)
            dst[pl.ds(g * G + pad, G)] = new.astype(BF16).reshape(G, C, N)

    wait_all(recv_sem.at[0], back3)
    temporal(back3, back2, bands_b, 2, PAD)
    temporal(back2, back1, bands_b, 1, PAD)
    temporal(back1, back0, bands_b, 0, 0)
    for k in range(Q):
        send_group(k, back0, grad_f, me, send_sem.at[2], recv_grad.at[k])
    grad_f[me] = back0[me]
    for b in range(3):
        bands_v[b] = banded([sw_ref[a, b] for a in range(3)], G + 2, [2 - a for a in range(3)], True, True)
        slopes[b, 0] = jnp.zeros((C, N), BF16)
        slopes[b, N + 1] = jnp.zeros((C, N), BF16)

    wait_all(recv_sem.at[1], st0)
    temporal(st0, st1, bands_f, 0, PAD)
    temporal(st1, st2, bands_f, 1, PAD)
    temporal(st2, st3, bands_f, 2, 0)

    def send_output(k):
        if k >= 3:
            wait_some(send_out.at[k - 3], st3, Z if k > 3 else Z - 1)
        send_group(k, st3, out_f, me, send_out.at[k], recv_out.at[k])

    for k in range(3):
        send_output(k)
    out_f[me] = st3[me]

    block = iota((C, 128), 1) >> 4
    last = jnp.zeros((C, 128), F32)
    packed = jnp.zeros((C, 128), F32)
    for layer, (state, back) in enumerate(((st0, back1), (st1, back2), (st2, back3))):
        e = 2**layer
        span = G + 2 * e
        acc_t[...] = jnp.zeros_like(acc_t)

        @pl.loop(0, GROUPS)
        def _(g):
            wide = state[pl.ds(g * G + PAD - e, span)].reshape(span * C, N)
            own = back[pl.ds(g * G + PAD, G)].reshape(G * C, N)
            acc_t[pl.ds(0, span * C)] += mm_nt(wide, own)

        for k in range(3):
            folded = fold(acc_t[pl.ds(0, span * C)], span, k * e)
            if layer * 3 + k < 8:
                packed = jnp.where(block == layer * 3 + k, folded, packed)
            else:
                last = jnp.where((block & 1) == 1, folded, last)
    packed_t = packed

    acc_s[...] = jnp.zeros_like(acc_s)

    @pl.loop(0, GROUPS)
    def _(k):
        wait_group(recv_grad.at[k], grad_f, k)
        g = lax.rem(q + Q - k, Q)
        rows = pl.ds(g * G, G)
        p = preact[rows].reshape(G * C, N)
        s = 1.0 / (1.0 + jnp.exp(-p))
        slope = grad_f[rows].reshape(G * C, N).astype(F32) * (s * (1.0 + p * (1.0 - s)))
        own = slope.astype(BF16)
        padded = pl.ds(g * G + 1, G)
        slopes[0, padded] = jnp.where(lane == N - 1, 0.0, pltpu.roll(slope, N - 1, 1)).astype(BF16).reshape(G, C, N)
        slopes[1, padded] = own.reshape(G, C, N)
        slopes[2, padded] = jnp.where(lane == 0, 0.0, pltpu.roll(slope, 1, 1)).astype(BF16).reshape(G, C, N)
        for b in range(3):
            acc_s[b] += mm_nt(xs[b, pl.ds(g * G, G + 2)].reshape((G + 2) * C, N), own)

    packed_s = jnp.zeros((C, 128), F32)
    for b in range(3):
        for a in range(3):
            folded = fold(acc_s[b], G + 2, a)
            if a * 3 + b < 8:
                packed_s = jnp.where(block == a * 3 + b, folded, packed_s)
            else:
                last = jnp.where((block & 1) == 0, folded, last)
    packed_l = jnp.zeros((4, 128), F32)
    for m in range(4):
        packed_l = jnp.where((block[:4] >> 1) == m, last[4 * m : 4 * m + 4], packed_l)
    for m in range(4):
        pack[m, :4] = packed_s[4 * m : 4 * m + 4]
        pack[m, 4:] = packed_l[m : m + 1]
        pack[m + 4, :4] = packed_t[4 * m : 4 * m + 4]
        pack[m + 4, 4:] = jnp.zeros((1, 128), F32)

    def to_columns(src_of, dst, index):
        for d in range(1, Q):
            other = lax.rem(q + d, Q)
            pltpu.make_async_remote_copy(
                src_ref=src_of(other), dst_ref=dst.at[q], send_sem=send_sem.at[index], recv_sem=recv_sem.at[index],
                device_id={"seq": other * Z + z}, device_id_type=MESH,
            ).start()

    def clip_gradient(g):
        total = jnp.zeros((C * G, N), F32)
        for b in range(3):
            total = total + mm(bands_v[b], slopes[b, pl.ds(g * G, G + 2)].reshape((G + 2) * C, N))
        grad_v[:, pl.ds(pl.multiple_of(g * G, G), G), :] = total.astype(BF16).reshape(C, G, N)

    to_columns(lambda other: pack.at[other], sum1, 3)
    sum1[q] = pack[q]
    send_output(3)

    @pl.loop(0, GROUPS // 2)
    def _(g):
        clip_gradient(g)

    wait_some(recv_sem.at[3], sum1, Q - 1)
    part1[...] = jnp.sum(sum1[...], axis=0)
    for d in range(1, Z):
        other = lax.rem(z + d, Z)
        pltpu.make_async_remote_copy(
            src_ref=part1, dst_ref=sum2.at[z], send_sem=send_sem.at[4], recv_sem=recv_sem.at[4],
            device_id={"seq": q * Z + other}, device_id_type=MESH,
        ).start()
    sum2[z] = part1[...]
    send_output(4)
    send_output(5)

    @pl.loop(GROUPS // 2, GROUPS)
    def _(g):
        clip_gradient(g)

    grad_store = pltpu.make_async_copy(grad_v, grad_hbm.at[0], local_sem.at[0])
    grad_store.start()
    send_output(6)

    wait_some(recv_sem.at[4], sum2, Z - 1)
    part2[...] = jnp.sum(sum2[...], axis=0)
    to_columns(lambda other: part2, sum3, 5)
    sum3[q] = part2[...]
    send_output(7)

    def output_rows(k):
        wait_group(recv_out.at[k], out_f, k)
        rows = pl.ds(pl.multiple_of(lax.rem(q + Q - k, Q) * G, G), G)
        out_v[:, rows, :] = mm(swap, out_f[rows].reshape(G * C, N)).astype(BF16).reshape(C, G, N)
        pltpu.make_async_copy(out_v.at[:, rows, :], out_hbm.at[0, :, rows, :], local_sem.at[1]).start()

    @pl.loop(0, GROUPS // 2)
    def _(k):
        output_rows(k)

    wait_some(recv_sem.at[5], sum3, Q - 1)
    for m in range(4):
        total[pl.ds(4 * m, 4)] = sum3[m, :4] * factor
        total[pl.ds(16 + 4 * m, 4)] = sum3[m + 4, :4] * factor
        total[pl.ds(32 + m, 1)] = sum3[m, 4:] * factor
    last = total[pl.ds(32, 4)]
    for tap in range(9):
        at = (128 - tap * C) % 128
        if tap < 8:
            sgrad_ref[tap // 3, tap % 3] = pltpu.roll(total[pl.ds(0, C)], at, 1)[:, :C] if at else total[pl.ds(0, C)][:, :C]
            tgrad_ref[tap // 3, tap % 3] = pltpu.roll(total[pl.ds(C, C)], at, 1)[:, :C] if at else total[pl.ds(C, C)][:, :C]
        else:
            for m in range(4):
                back_by = (128 - 32 * m) % 128
                sgrad_ref[2, 2, pl.ds(4 * m, 4)] = (pltpu.roll(last, back_by, 1) if back_by else last)[:, :C]
                tgrad_ref[2, 2, pl.ds(4 * m, 4)] = pltpu.roll(last, back_by - C if m else 128 - C, 1)[:, :C]

    @pl.loop(GROUPS // 2, GROUPS)
    def _(k):
        output_rows(k)

    for index, ref in enumerate((cot_f, act_f, back0)):
        wait_all(send_sem.at[index], ref)
    for k in range(5, Q):
        wait_some(send_out.at[k], st3, Z)
    wait_some(send_sem.at[3], sum1, Q - 1)
    wait_some(send_sem.at[4], sum2, Z - 1)
    wait_some(send_sem.at[5], sum3, Q - 1)
    grad_store.wait()
    pltpu.make_async_copy(out_v, out_hbm.at[0], local_sem.at[1]).wait()


def hand_over(*refs):
    count = (len(refs) - 1) // 2
    sems = refs[-1]
    copies = [pltpu.make_async_copy(refs[n], refs[count + n], sems.at[n]) for n in range(count)]
    for copy in copies:
        copy.start()
    for copy in copies:
        copy.wait()


def body(clip_frames, cotangent, spatial_weight, temporal_weight):
    factor = 1.0 / math.sqrt(N * N * N)
    vmem = pl.BlockSpec(memory_space=pltpu.VMEM)
    anywhere = pl.BlockSpec(memory_space=pltpu.HBM)
    frame = pltpu.VMEM((N, C, N), BF16)
    padded = pltpu.VMEM((N + 2 * PAD, C, N), BF16)
    results = pl.pallas_call(
        functools.partial(kernel, factor),
        out_shape=(
            jax.ShapeDtypeStruct((1, C, N, N), BF16),
            jax.ShapeDtypeStruct((1, C, N, N), BF16),
            jax.ShapeDtypeStruct((3, 3, C, C), F32),
            jax.ShapeDtypeStruct((3, 3, C, C), F32),
        ),
        in_specs=[anywhere] * 4,
        out_specs=(anywhere, anywhere, vmem, vmem),
        scratch_shapes=[
            pltpu.VMEM((3, 3, C, C), BF16),
            pltpu.VMEM((3, 3, C, C), BF16),
            pltpu.VMEM((C, N, N), BF16),
            pltpu.VMEM((C, N, N), BF16),
            frame,
            frame,
            pltpu.VMEM((3, N + 2, C, N), BF16),
            pltpu.VMEM((N, C, N), F32),
            pltpu.VMEM((3, G * C, (G + 2) * C), BF16),
            pltpu.VMEM((3, G * C, (G + 2) * C), BF16),
            pltpu.VMEM((3, G * C, (G + 8) * C), BF16),
            pltpu.VMEM((3, G * C, (G + 8) * C), BF16),
            padded, padded, padded, frame,
            padded, padded, padded, frame,
            frame,
            frame,
            pltpu.VMEM((3, N + 2, C, N), BF16),
            pltpu.VMEM(((G + 8) * C, G * C), F32),
            pltpu.VMEM((3, (G + 2) * C, G * C), F32),
            pltpu.VMEM((Q, PIECE, 128), F32),
            pltpu.VMEM((Q, PIECE, 128), F32),
            pltpu.VMEM((PIECE, 128), F32),
            pltpu.VMEM((Z, PIECE, 128), F32),
            pltpu.VMEM((PIECE, 128), F32),
            pltpu.VMEM((Q, PIECE, 128), F32),
            pltpu.VMEM((40, 128), F32),
            pltpu.VMEM((C, N, N), BF16),
            pltpu.VMEM((C, N, N), BF16),
            pltpu.SemaphoreType.DMA((4,)),
            pltpu.SemaphoreType.DMA((6,)),
            pltpu.SemaphoreType.DMA((6,)),
            pltpu.SemaphoreType.DMA((Q,)),
            pltpu.SemaphoreType.DMA((Q,)),
            pltpu.SemaphoreType.DMA((Q,)),
            pltpu.SemaphoreType.REGULAR,
        ],
        compiler_params=pltpu.CompilerParams(collective_id=0, has_side_effects=True, vmem_limit_bytes=VMEM_LIMIT),
    )(clip_frames, cotangent, spatial_weight, temporal_weight)
    return pl.pallas_call(
        hand_over,
        out_shape=tuple(jax.ShapeDtypeStruct(r.shape, r.dtype) for r in results),
        in_specs=[anywhere] * 4,
        out_specs=(anywhere,) * 4,
        scratch_shapes=[pltpu.SemaphoreType.DMA((4,))],
        compiler_params=pltpu.CompilerParams(vmem_limit_bytes=VMEM_LIMIT),
    )(*results)


def solution(mesh):
    placed = (P(("dp", "seq"), None, None, None), P(("dp", "seq"), None, None, None), P(), P())
    return jax.shard_map(
        body,
        mesh=mesh,
        in_specs=placed,
        out_specs=(
            P(("dp", "seq"), None, None, None),
            P(("dp", "seq"), None, None, None),
            P("dp", None, None, None),
            P("dp", None, None, None),
        ),
        check_vma=False,
    )
```

```python
import functools
import math

import jax
import jax.numpy as jnp
from jax import lax
from jax.experimental import pallas as pl
from jax.experimental.pallas import tpu as pltpu
from jax.sharding import PartitionSpec as P

MESH = pl.DeviceIdType.MESH
F32 = jnp.float32
BF16 = jnp.bfloat16
C = 16
N = 128
SEQ = 128
Z = 16
Q = SEQ // Z
G = 16
GROUPS = N // G
PAD = 4
PIECE = 5
VMEM_LIMIT = 60 << 20
HANDED = 4


def iota(shape, axis):
    return lax.broadcasted_iota(jnp.int32, shape, axis)


def mm(a, b):
    return lax.dot_general(a, b, (((1,), (0,)), ((), ())), preferred_element_type=F32)


def mm_nt(a, b):
    return lax.dot_general(a, b, (((1,), (1,)), ((), ())), preferred_element_type=F32)


def one_hot(cond):
    return jnp.where(cond, 1.0, 0.0).astype(BF16)


def banded(weights, span, offsets, transposed, out_channel_major=False):
    cols = span * C
    i = iota((G * C, cols), 0)
    j = iota((G * C, cols), 1)
    si = iota((G * C, C), 0)
    sj = iota((G * C, C), 1)
    if out_channel_major:
        place = i & (G - 1)
        spread = one_hot((si >> 4) == sj)
    else:
        place = i >> 4
        spread = one_hot((si & (C - 1)) == sj)
    tile = one_hot(iota((C, cols), 0) == (iota((C, cols), 1) & (C - 1)))
    diff = (j >> 4) - place
    total = jnp.zeros((G * C, cols), F32)
    for weight, offset in zip(weights, offsets):
        rows = (mm if transposed else mm_nt)(spread, weight).astype(BF16)
        total = jnp.where(diff == offset, mm(rows, tile), total)
    return total.astype(BF16)


def fold(acc, span, offset):
    rows = span * C
    diff = (iota((rows, G * C), 0) >> 4) - (iota((rows, G * C), 1) >> 4)
    kept = jnp.where(diff == offset, acc, 0.0)
    total = jnp.sum(kept.reshape(span, C, G * C), axis=0)
    total = total[:, :128] + total[:, 128:]
    for step in (64, 32, 16):
        total = total + pltpu.roll(total, step, 1)
    return total


def kernel(
    factor,
    clip_hbm, cot_hbm, sw_hbm, tw_hbm,
    out_hbm, grad_hbm, sgrad_ref, tgrad_ref,
    sw_ref, tw_ref, clip_in, cot_in, cot_f, act_f, xs, preact, bands_s, bands_v, bands_f, bands_b,
    back3, back2, back1, back0, st0, st1, st2, st3, grad_f, out_f, slopes,
    acc_t, acc_s, pack, sum1, part1, sum2, part2, sum3, total, out_v, grad_v,
    local_sem, send_sem, recv_sem, send_out, recv_grad, recv_out, ready,
):
    me = lax.axis_index("seq")
    q, z = me // Z, lax.rem(me, Z)

    cot_load = pltpu.make_async_copy(cot_hbm.at[0], cot_in, local_sem.at[0])
    cot_load.start()
    clip_load = pltpu.make_async_copy(clip_hbm.at[0], clip_in, local_sem.at[1])
    clip_load.start()
    sw_load = pltpu.make_async_copy(sw_hbm, sw_ref, local_sem.at[2])
    sw_load.start()
    tw_load = pltpu.make_async_copy(tw_hbm, tw_ref, local_sem.at[3])
    tw_load.start()

    barrier = pltpu.get_barrier_semaphore()
    for d in range(1, Q):
        pl.semaphore_signal(barrier, inc=1, device_id={"seq": lax.rem(q + d, Q) * Z + z}, device_id_type=MESH)
    for d in range(1, Z):
        pl.semaphore_signal(barrier, inc=1, device_id={"seq": q * Z + lax.rem(z + d, Z)}, device_id_type=MESH)

    def send_group(k, src, dst, at, sent, received):
        column = lax.rem(q + k, Q) * Z

        def send(i):
            j = 8 + lax.rem(i, 2) * (i + 1) // 2 - (1 - lax.rem(i, 2)) * (i // 2)
            t = column + lax.rem(z + j, Z)
            pltpu.make_async_remote_copy(
                src_ref=src.at[t], dst_ref=dst.at[at], send_sem=sent, recv_sem=received,
                device_id={"seq": t}, device_id_type=MESH,
            ).start()

        @pl.loop(0, Z if k else Z - 1)
        def _(i):
            send(i)

    def send_all(index, src, dst, at):
        for k in range(Q):
            send_group(k, src, dst, at, send_sem.at[index], recv_sem.at[index])

    def wait_some(sem, ref, count):
        part = ref.at[pl.ds(0, count)]
        pltpu.make_async_copy(part, part, sem).wait()

    def wait_all(sem, ref):
        wait_some(sem, ref, SEQ - 1)

    def wait_group(sem, ref, k):
        @pl.when(k == 0)
        def _():
            wait_some(sem, ref, Z - 1)

        @pl.when(k > 0)
        def _():
            wait_some(sem, ref, Z)

    i = iota((G * C, G * C), 0)
    j = iota((G * C, G * C), 1)
    swap = one_hot(((i & (C - 1)) == (j >> 4)) & ((i >> 4) == (j & (G - 1))))

    cot_load.wait()

    def cotangent_rows(k):
        rows = pl.ds(pl.multiple_of(lax.rem(q + k, Q) * G, G), G)
        cot_f[rows] = mm(swap, cot_in[:, rows, :].reshape(C * G, N)).astype(BF16).reshape(G, C, N)

    cotangent_rows(0)
    pl.semaphore_wait(barrier, Q - 1 + Z - 1)
    for d in range(1, Z):
        pl.semaphore_signal(ready, inc=1, device_id={"seq": q * Z + lax.rem(z + d, Z)}, device_id_type=MESH)
    send_group(0, cot_f, back3, me + PAD, send_sem.at[0], recv_sem.at[0])
    back3[me + PAD] = cot_f[me]

    @pl.loop(1, Q)
    def _(k):
        cotangent_rows(k)

    pl.semaphore_wait(ready, Z - 1)
    for k in range(1, Q):
        send_group(k, cot_f, back3, me + PAD, send_sem.at[0], recv_sem.at[0])

    clip_load.wait()
    sw_load.wait()
    tw_load.wait()
    for b in range(3):
        bands_s[b] = banded([sw_ref[a, b] for a in range(3)], G + 2, range(3), False)
        xs[b, 0] = jnp.zeros((C, N), BF16)
        xs[b, N + 1] = jnp.zeros((C, N), BF16)
    lane = iota((G * C, N), 1)

    @pl.loop(0, GROUPS)
    def _(g):
        rows = pl.ds(pl.multiple_of(g * G, G), G)
        x = mm(swap, clip_in[:, rows, :].reshape(C * G, N))
        padded = pl.ds(g * G + 1, G)
        xs[0, padded] = jnp.where(lane == 0, 0.0, pltpu.roll(x, 1, 1)).astype(BF16).reshape(G, C, N)
        xs[1, padded] = x.astype(BF16).reshape(G, C, N)
        xs[2, padded] = jnp.where(lane == N - 1, 0.0, pltpu.roll(x, N - 1, 1)).astype(BF16).reshape(G, C, N)

    @pl.loop(0, GROUPS)
    def _(g):
        p = jnp.zeros((G * C, N), F32)
        for b in range(3):
            p = p + mm(bands_s[b], xs[b, pl.ds(g * G, G + 2)].reshape((G + 2) * C, N))
        rows = pl.ds(g * G, G)
        preact[rows] = p.reshape(G, C, N)
        act_f[rows] = (p / (1.0 + jnp.exp(-p))).astype(BF16).reshape(G, C, N)

    send_all(1, act_f, st0, me + PAD)
    st0[me + PAD] = act_f[me]

    zeros = jnp.zeros((PAD, C, N), BF16)
    for ref in (back3, back2, back1, st0, st1, st2):
        ref[pl.ds(0, PAD)] = zeros
        ref[pl.ds(N + PAD, PAD)] = zeros
    for layer in range(3):
        e = 2**layer
        span = G + 2 * e
        taps = [tw_ref[layer, k] for k in range(3)]
        bands_b[layer, :, pl.ds(0, span * C)] = banded(taps, span, [(2 - k) * e for k in range(3)], True)
        bands_f[layer, :, pl.ds(0, span * C)] = banded(taps, span, [k * e for k in range(3)], False)

    def temporal(src, dst, bands, layer, pad):
        e = 2**layer
        span = G + 2 * e

        @pl.loop(0, GROUPS)
        def _(g):
            own = src[pl.ds(g * G + PAD, G)].reshape(G * C, N).astype(F32)
            wide = src[pl.ds(g * G + PAD - e, span)].reshape(span * C, N)
            new = own + mm(bands[layer, :, pl.ds(0, span * C)], wide)
            dst[pl.ds(g * G + pad, G)] = new.astype(BF16).reshape(G, C, N)

    wait_all(recv_sem.at[0], back3)
    temporal(back3, back2, bands_b, 2, PAD)
    temporal(back2, back1, bands_b, 1, PAD)
    temporal(back1, back0, bands_b, 0, 0)
    for k in range(Q):
        send_group(k, back0, grad_f, me, send_sem.at[2], recv_grad.at[k])
    grad_f[me] = back0[me]
    for b in range(3):
        bands_v[b] = banded([sw_ref[a, b] for a in range(3)], G + 2, [2 - a for a in range(3)], True, True)
        slopes[b, 0] = jnp.zeros((C, N), BF16)
        slopes[b, N + 1] = jnp.zeros((C, N), BF16)

    wait_all(recv_sem.at[1], st0)
    temporal(st0, st1, bands_f, 0, PAD)
    temporal(st1, st2, bands_f, 1, PAD)
    temporal(st2, st3, bands_f, 2, 0)

    def send_output(k):
        if k >= 3:
            wait_some(send_out.at[k - 3], st3, Z if k > 3 else Z - 1)
        send_group(k, st3, out_f, me, send_out.at[k], recv_out.at[k])

    for k in range(3):
        send_output(k)
    out_f[me] = st3[me]

    block = iota((C, 128), 1) >> 4
    last = jnp.zeros((C, 128), F32)
    packed = jnp.zeros((C, 128), F32)
    for layer, (state, back) in enumerate(((st0, back1), (st1, back2), (st2, back3))):
        e = 2**layer
        span = G + 2 * e
        acc_t[...] = jnp.zeros_like(acc_t)

        @pl.loop(0, GROUPS)
        def _(g):
            wide = state[pl.ds(g * G + PAD - e, span)].reshape(span * C, N)
            own = back[pl.ds(g * G + PAD, G)].reshape(G * C, N)
            acc_t[pl.ds(0, span * C)] += mm_nt(wide, own)

        for k in range(3):
            folded = fold(acc_t[pl.ds(0, span * C)], span, k * e)
            if layer * 3 + k < 8:
                packed = jnp.where(block == layer * 3 + k, folded, packed)
            else:
                last = jnp.where((block & 1) == 1, folded, last)
    packed_t = packed

    acc_s[...] = jnp.zeros_like(acc_s)

    @pl.loop(0, GROUPS)
    def _(k):
        wait_group(recv_grad.at[k], grad_f, k)
        g = lax.rem(q + Q - k, Q)
        rows = pl.ds(g * G, G)
        p = preact[rows].reshape(G * C, N)
        s = 1.0 / (1.0 + jnp.exp(-p))
        slope = grad_f[rows].reshape(G * C, N).astype(F32) * (s * (1.0 + p * (1.0 - s)))
        own = slope.astype(BF16)
        padded = pl.ds(g * G + 1, G)
        slopes[0, padded] = jnp.where(lane == N - 1, 0.0, pltpu.roll(slope, N - 1, 1)).astype(BF16).reshape(G, C, N)
        slopes[1, padded] = own.reshape(G, C, N)
        slopes[2, padded] = jnp.where(lane == 0, 0.0, pltpu.roll(slope, 1, 1)).astype(BF16).reshape(G, C, N)
        for b in range(3):
            acc_s[b] += mm_nt(xs[b, pl.ds(g * G, G + 2)].reshape((G + 2) * C, N), own)

    packed_s = jnp.zeros((C, 128), F32)
    for b in range(3):
        for a in range(3):
            folded = fold(acc_s[b], G + 2, a)
            if a * 3 + b < 8:
                packed_s = jnp.where(block == a * 3 + b, folded, packed_s)
            else:
                last = jnp.where((block & 1) == 0, folded, last)
    packed_l = jnp.zeros((4, 128), F32)
    for m in range(4):
        packed_l = jnp.where((block[:4] >> 1) == m, last[4 * m : 4 * m + 4], packed_l)
    for m in range(4):
        pack[m, :4] = packed_s[4 * m : 4 * m + 4]
        pack[m, 4:] = packed_l[m : m + 1]
        pack[m + 4, :4] = packed_t[4 * m : 4 * m + 4]
        pack[m + 4, 4:] = jnp.zeros((1, 128), F32)

    def to_columns(src_of, dst, index):
        for d in range(1, Q):
            other = lax.rem(q + d, Q)
            pltpu.make_async_remote_copy(
                src_ref=src_of(other), dst_ref=dst.at[q], send_sem=send_sem.at[index], recv_sem=recv_sem.at[index],
                device_id={"seq": other * Z + z}, device_id_type=MESH,
            ).start()

    def clip_gradient(g):
        total = jnp.zeros((C * G, N), F32)
        for b in range(3):
            total = total + mm(bands_v[b], slopes[b, pl.ds(g * G, G + 2)].reshape((G + 2) * C, N))
        grad_v[:, pl.ds(pl.multiple_of(g * G, G), G), :] = total.astype(BF16).reshape(C, G, N)

    to_columns(lambda other: pack.at[other], sum1, 3)
    sum1[q] = pack[q]
    send_output(3)

    @pl.loop(0, GROUPS // 2)
    def _(g):
        clip_gradient(g)

    wait_some(recv_sem.at[3], sum1, Q - 1)
    part1[...] = jnp.sum(sum1[...], axis=0)
    for d in range(1, Z):
        other = lax.rem(z + d, Z)
        pltpu.make_async_remote_copy(
            src_ref=part1, dst_ref=sum2.at[z], send_sem=send_sem.at[4], recv_sem=recv_sem.at[4],
            device_id={"seq": q * Z + other}, device_id_type=MESH,
        ).start()
    sum2[z] = part1[...]
    send_output(4)
    send_output(5)

    @pl.loop(GROUPS // 2, GROUPS)
    def _(g):
        clip_gradient(g)

    grad_store = pltpu.make_async_copy(grad_v, grad_hbm.at[0], local_sem.at[0])
    grad_store.start()
    send_output(6)

    wait_some(recv_sem.at[4], sum2, Z - 1)
    part2[...] = jnp.sum(sum2[...], axis=0)
    to_columns(lambda other: part2, sum3, 5)
    sum3[q] = part2[...]
    send_output(7)

    def output_rows(k):
        wait_group(recv_out.at[k], out_f, k)
        rows = pl.ds(pl.multiple_of(lax.rem(q + Q - k, Q) * G, G), G)
        out_v[:, rows, :] = mm(swap, out_f[rows].reshape(G * C, N)).astype(BF16).reshape(C, G, N)
        pltpu.make_async_copy(out_v.at[:, rows, :], out_hbm.at[0, :, rows, :], local_sem.at[1]).start()

    @pl.loop(0, GROUPS // 2)
    def _(k):
        output_rows(k)

    wait_some(recv_sem.at[5], sum3, Q - 1)
    for m in range(4):
        total[pl.ds(4 * m, 4)] = sum3[m, :4] * factor
        total[pl.ds(16 + 4 * m, 4)] = sum3[m + 4, :4] * factor
        total[pl.ds(32 + m, 1)] = sum3[m, 4:] * factor
    last = total[pl.ds(32, 4)]
    for tap in range(9):
        at = (128 - tap * C) % 128
        if tap < 8:
            sgrad_ref[tap // 3, tap % 3] = pltpu.roll(total[pl.ds(0, C)], at, 1)[:, :C] if at else total[pl.ds(0, C)][:, :C]
            tgrad_ref[tap // 3, tap % 3] = pltpu.roll(total[pl.ds(C, C)], at, 1)[:, :C] if at else total[pl.ds(C, C)][:, :C]
        else:
            for m in range(4):
                back_by = (128 - 32 * m) % 128
                sgrad_ref[2, 2, pl.ds(4 * m, 4)] = (pltpu.roll(last, back_by, 1) if back_by else last)[:, :C]
                tgrad_ref[2, 2, pl.ds(4 * m, 4)] = pltpu.roll(last, back_by - C if m else 128 - C, 1)[:, :C]

    @pl.loop(GROUPS // 2, GROUPS)
    def _(k):
        output_rows(k)

    for index, ref in enumerate((cot_f, act_f, back0)):
        wait_all(send_sem.at[index], ref)
    for k in range(5, Q):
        wait_some(send_out.at[k], st3, Z)
    wait_some(send_sem.at[3], sum1, Q - 1)
    wait_some(send_sem.at[4], sum2, Z - 1)
    wait_some(send_sem.at[5], sum3, Q - 1)
    grad_store.wait()
    pltpu.make_async_copy(out_v, out_hbm.at[0], local_sem.at[1]).wait()


def hand_over(out_in, grad_in, sgrad_in, tgrad_in, out_hbm, grad_hbm, sgrad_hbm, tgrad_hbm, *scratch):
    stages, load_sem, store_sem = scratch[:4], scratch[4], scratch[5]
    loads, stores = [], []
    pairs = zip((out_in, grad_in, sgrad_in, tgrad_in), stages, (out_hbm, grad_hbm, sgrad_hbm, tgrad_hbm))
    for source, stage, target in pairs:
        for part in range(HANDED if source.shape[0] == 1 else 1):
            at = (0, pl.ds(part * C // HANDED, C // HANDED)) if source.shape[0] == 1 else slice(None)
            loads.append(pltpu.make_async_copy(source.at[at], stage.at[at], load_sem.at[len(loads)]))
            stores.append(pltpu.make_async_copy(stage.at[at], target.at[at], store_sem.at[len(stores)]))
    for load in loads:
        load.start()
    for load, store in zip(loads, stores):
        load.wait()
        store.start()
    for store in stores:
        store.wait()


def body(clip_frames, cotangent, spatial_weight, temporal_weight):
    factor = 1.0 / math.sqrt(N * N * N)
    vmem = pl.BlockSpec(memory_space=pltpu.VMEM)
    anywhere = pl.BlockSpec(memory_space=pltpu.HBM)
    frame = pltpu.VMEM((N, C, N), BF16)
    padded = pltpu.VMEM((N + 2 * PAD, C, N), BF16)
    results = pl.pallas_call(
        functools.partial(kernel, factor),
        out_shape=(
            jax.ShapeDtypeStruct((1, C, N, N), BF16),
            jax.ShapeDtypeStruct((1, C, N, N), BF16),
            jax.ShapeDtypeStruct((3, 3, C, C), F32),
            jax.ShapeDtypeStruct((3, 3, C, C), F32),
        ),
        in_specs=[anywhere] * 4,
        out_specs=(anywhere, anywhere, vmem, vmem),
        scratch_shapes=[
            pltpu.VMEM((3, 3, C, C), BF16),
            pltpu.VMEM((3, 3, C, C), BF16),
            pltpu.VMEM((C, N, N), BF16),
            pltpu.VMEM((C, N, N), BF16),
            frame,
            frame,
            pltpu.VMEM((3, N + 2, C, N), BF16),
            pltpu.VMEM((N, C, N), F32),
            pltpu.VMEM((3, G * C, (G + 2) * C), BF16),
            pltpu.VMEM((3, G * C, (G + 2) * C), BF16),
            pltpu.VMEM((3, G * C, (G + 8) * C), BF16),
            pltpu.VMEM((3, G * C, (G + 8) * C), BF16),
            padded, padded, padded, frame,
            padded, padded, padded, frame,
            frame,
            frame,
            pltpu.VMEM((3, N + 2, C, N), BF16),
            pltpu.VMEM(((G + 8) * C, G * C), F32),
            pltpu.VMEM((3, (G + 2) * C, G * C), F32),
            pltpu.VMEM((Q, PIECE, 128), F32),
            pltpu.VMEM((Q, PIECE, 128), F32),
            pltpu.VMEM((PIECE, 128), F32),
            pltpu.VMEM((Z, PIECE, 128), F32),
            pltpu.VMEM((PIECE, 128), F32),
            pltpu.VMEM((Q, PIECE, 128), F32),
            pltpu.VMEM((40, 128), F32),
            pltpu.VMEM((C, N, N), BF16),
            pltpu.VMEM((C, N, N), BF16),
            pltpu.SemaphoreType.DMA((4,)),
            pltpu.SemaphoreType.DMA((6,)),
            pltpu.SemaphoreType.DMA((6,)),
            pltpu.SemaphoreType.DMA((Q,)),
            pltpu.SemaphoreType.DMA((Q,)),
            pltpu.SemaphoreType.DMA((Q,)),
            pltpu.SemaphoreType.REGULAR,
        ],
        compiler_params=pltpu.CompilerParams(collective_id=0, has_side_effects=True, vmem_limit_bytes=VMEM_LIMIT),
    )(clip_frames, cotangent, spatial_weight, temporal_weight)
    return pl.pallas_call(
        hand_over,
        out_shape=tuple(jax.ShapeDtypeStruct(r.shape, r.dtype) for r in results),
        in_specs=[anywhere] * 4,
        out_specs=(anywhere,) * 4,
        scratch_shapes=[pltpu.VMEM(r.shape, r.dtype) for r in results] + [pltpu.SemaphoreType.DMA((2 * HANDED + 2,))] * 2,
        compiler_params=pltpu.CompilerParams(vmem_limit_bytes=VMEM_LIMIT),
    )(*results)


def solution(mesh):
    placed = (P(("dp", "seq"), None, None, None), P(("dp", "seq"), None, None, None), P(), P())
    return jax.shard_map(
        body,
        mesh=mesh,
        in_specs=placed,
        out_specs=(
            P(("dp", "seq"), None, None, None),
            P(("dp", "seq"), None, None, None),
            P("dp", None, None, None),
            P("dp", None, None, None),
        ),
        check_vma=False,
    )
```

```python
import functools
import math

import jax
import jax.numpy as jnp
from jax import lax
from jax.experimental import pallas as pl
from jax.experimental.pallas import tpu as pltpu
from jax.sharding import PartitionSpec as P

MESH = pl.DeviceIdType.MESH
F32 = jnp.float32
BF16 = jnp.bfloat16
C = 16
N = 128
SEQ = 128
Z = 16
Q = SEQ // Z
G = 16
GROUPS = N // G
PAD = 4
PIECE = 5
VMEM_LIMIT = 60 << 20
HANDED = 4


def iota(shape, axis):
    return lax.broadcasted_iota(jnp.int32, shape, axis)


def mm(a, b):
    return lax.dot_general(a, b, (((1,), (0,)), ((), ())), preferred_element_type=F32)


def mm_nt(a, b):
    return lax.dot_general(a, b, (((1,), (1,)), ((), ())), preferred_element_type=F32)


def one_hot(cond):
    return jnp.where(cond, 1.0, 0.0).astype(BF16)


def banded(weights, span, offsets, transposed, out_channel_major=False):
    cols = span * C
    i = iota((G * C, cols), 0)
    j = iota((G * C, cols), 1)
    si = iota((G * C, C), 0)
    sj = iota((G * C, C), 1)
    if out_channel_major:
        place = i & (G - 1)
        spread = one_hot((si >> 4) == sj)
    else:
        place = i >> 4
        spread = one_hot((si & (C - 1)) == sj)
    tile = one_hot(iota((C, cols), 0) == (iota((C, cols), 1) & (C - 1)))
    diff = (j >> 4) - place
    total = jnp.zeros((G * C, cols), F32)
    for weight, offset in zip(weights, offsets):
        rows = (mm if transposed else mm_nt)(spread, weight).astype(BF16)
        total = jnp.where(diff == offset, mm(rows, tile), total)
    return total.astype(BF16)


def fold(acc, span, offset):
    rows = span * C
    diff = (iota((rows, G * C), 0) >> 4) - (iota((rows, G * C), 1) >> 4)
    kept = jnp.where(diff == offset, acc, 0.0)
    total = jnp.sum(kept.reshape(span, C, G * C), axis=0)
    total = total[:, :128] + total[:, 128:]
    for step in (64, 32, 16):
        total = total + pltpu.roll(total, step, 1)
    return total


def kernel(
    factor,
    clip_hbm, cot_hbm, sw_hbm, tw_hbm,
    out_hbm, grad_hbm, sgrad_ref, tgrad_ref,
    sw_ref, tw_ref, clip_in, cot_in, cot_f, cot_z, act_f, xs, preact, bands_s, bands_v, bands_f, bands_b,
    back3, back2, back1, back0, st0, st1, st2, st3, grad_f, out_f, slopes,
    acc_t, acc_s, pack, sum1, part1, sum2, part2, sum3, total, out_v, grad_v,
    local_sem, send_sem, recv_sem, send_act, send_out, recv_grad, recv_out, ready,
):
    me = lax.axis_index("seq")
    q, z = me // Z, lax.rem(me, Z)

    cot_load = pltpu.make_async_copy(cot_hbm.at[0], cot_in, local_sem.at[0])
    cot_load.start()
    clip_load = pltpu.make_async_copy(clip_hbm.at[0], clip_in, local_sem.at[1])
    clip_load.start()
    sw_load = pltpu.make_async_copy(sw_hbm, sw_ref, local_sem.at[2])
    sw_load.start()
    tw_load = pltpu.make_async_copy(tw_hbm, tw_ref, local_sem.at[3])
    tw_load.start()

    barrier = pltpu.get_barrier_semaphore()
    for d in range(1, Q):
        pl.semaphore_signal(barrier, inc=1, device_id={"seq": lax.rem(q + d, Q) * Z + z}, device_id_type=MESH)
    for d in range(1, Z):
        pl.semaphore_signal(barrier, inc=1, device_id={"seq": q * Z + lax.rem(z + d, Z)}, device_id_type=MESH)

    def send_group(k, src, dst, at, sent, received):
        column = lax.rem(q + k, Q) * Z

        def send(i):
            j = 8 + lax.rem(i, 2) * (i + 1) // 2 - (1 - lax.rem(i, 2)) * (i // 2)
            t = column + lax.rem(z + j, Z)
            pltpu.make_async_remote_copy(
                src_ref=src.at[t], dst_ref=dst.at[at], send_sem=sent, recv_sem=received,
                device_id={"seq": t}, device_id_type=MESH,
            ).start()

        @pl.loop(0, Z if k else Z - 1)
        def _(i):
            send(i)

    def wait_some(sem, ref, count):
        part = ref.at[pl.ds(0, count)]
        pltpu.make_async_copy(part, part, sem).wait()

    def wait_all(sem, ref):
        wait_some(sem, ref, SEQ - 1)

    def wait_group(sem, ref, k):
        @pl.when(k == 0)
        def _():
            wait_some(sem, ref, Z - 1)

        @pl.when(k > 0)
        def _():
            wait_some(sem, ref, Z)

    i = iota((G * C, G * C), 0)
    j = iota((G * C, G * C), 1)
    swap = one_hot(((i & (C - 1)) == (j >> 4)) & ((i >> 4) == (j & (G - 1))))

    cot_load.wait()

    @pl.loop(0, GROUPS)
    def _(g):
        rows = pl.ds(pl.multiple_of(g * G, G), G)
        cot_f[g] = mm(swap, cot_in[:, rows, :].reshape(C * G, N)).astype(BF16).reshape(G, C, N)

    pl.semaphore_wait(barrier, Q - 1 + Z - 1)

    @pl.loop(1, Z)
    def _(d):
        other = lax.rem(z + d, Z)
        pltpu.make_async_remote_copy(
            src_ref=cot_f.at[:, other], dst_ref=cot_z.at[z], send_sem=send_sem.at[0], recv_sem=recv_sem.at[0],
            device_id={"seq": q * Z + other}, device_id_type=MESH,
        ).start()

    for d in range(1, Z):
        pl.semaphore_signal(ready, inc=1, device_id={"seq": q * Z + lax.rem(z + d, Z)}, device_id_type=MESH)
    cot_z[z] = cot_f[:, z]

    clip_load.wait()
    sw_load.wait()
    tw_load.wait()
    for b in range(3):
        bands_s[b] = banded([sw_ref[a, b] for a in range(3)], G + 2, range(3), False)
        xs[b, 0] = jnp.zeros((C, N), BF16)
        xs[b, N + 1] = jnp.zeros((C, N), BF16)
    lane = iota((G * C, N), 1)

    @pl.loop(0, GROUPS)
    def _(g):
        rows = pl.ds(pl.multiple_of(g * G, G), G)
        x = mm(swap, clip_in[:, rows, :].reshape(C * G, N))
        padded = pl.ds(g * G + 1, G)
        xs[0, padded] = jnp.where(lane == 0, 0.0, pltpu.roll(x, 1, 1)).astype(BF16).reshape(G, C, N)
        xs[1, padded] = x.astype(BF16).reshape(G, C, N)
        xs[2, padded] = jnp.where(lane == N - 1, 0.0, pltpu.roll(x, N - 1, 1)).astype(BF16).reshape(G, C, N)

    @pl.loop(0, GROUPS)
    def _(g):
        p = jnp.zeros((G * C, N), F32)
        for b in range(3):
            p = p + mm(bands_s[b], xs[b, pl.ds(g * G, G + 2)].reshape((G + 2) * C, N))
        rows = pl.ds(g * G, G)
        preact[rows] = p.reshape(G, C, N)
        act_f[rows] = (p / (1.0 + jnp.exp(-p))).astype(BF16).reshape(G, C, N)

    pl.semaphore_wait(ready, Z - 1)

    def send_activated(k):
        if k >= 3:
            wait_some(send_act.at[k - 3], act_f, Z if k > 3 else Z - 1)
        send_group(k, act_f, st0, me + PAD, send_act.at[k], recv_sem.at[1])

    for k in range(3):
        send_activated(k)
    st0[me + PAD] = act_f[me]

    zeros = jnp.zeros((PAD, C, N), BF16)
    for ref in (back3, back2, back1, st0, st1, st2):
        ref[pl.ds(0, PAD)] = zeros
        ref[pl.ds(N + PAD, PAD)] = zeros
    for layer in range(3):
        e = 2**layer
        span = G + 2 * e
        taps = [tw_ref[layer, k] for k in range(3)]
        bands_b[layer, :, pl.ds(0, span * C)] = banded(taps, span, [(2 - k) * e for k in range(3)], True)
        bands_f[layer, :, pl.ds(0, span * C)] = banded(taps, span, [k * e for k in range(3)], False)

    def temporal(src, dst, bands, layer, pad):
        e = 2**layer
        span = G + 2 * e

        @pl.loop(0, GROUPS)
        def _(g):
            own = src[pl.ds(g * G + PAD, G)].reshape(G * C, N).astype(F32)
            wide = src[pl.ds(g * G + PAD - e, span)].reshape(span * C, N)
            new = own + mm(bands[layer, :, pl.ds(0, span * C)], wide)
            dst[pl.ds(g * G + pad, G)] = new.astype(BF16).reshape(G, C, N)

    wait_some(recv_sem.at[0], cot_z, Z - 1)
    own_frames = pl.ds(q * Z + PAD, Z)
    for k in range(1, Q):
        other = lax.rem(q + k, Q)
        pltpu.make_async_remote_copy(
            src_ref=cot_z.at[:, other], dst_ref=back3.at[own_frames], send_sem=send_sem.at[2], recv_sem=recv_sem.at[2],
            device_id={"seq": other * Z + z}, device_id_type=MESH,
        ).start()
    back3[own_frames] = cot_z[:, q]
    for k in range(3, Q):
        send_activated(k)

    wait_some(recv_sem.at[2], back3, SEQ - Z)
    temporal(back3, back2, bands_b, 2, PAD)
    temporal(back2, back1, bands_b, 1, PAD)
    temporal(back1, back0, bands_b, 0, 0)
    for k in range(Q):
        send_group(k, back0, grad_f, me, send_sem.at[1], recv_grad.at[k])
    grad_f[me] = back0[me]
    for b in range(3):
        bands_v[b] = banded([sw_ref[a, b] for a in range(3)], G + 2, [2 - a for a in range(3)], True, True)
        slopes[b, 0] = jnp.zeros((C, N), BF16)
        slopes[b, N + 1] = jnp.zeros((C, N), BF16)

    wait_all(recv_sem.at[1], st0)
    temporal(st0, st1, bands_f, 0, PAD)
    temporal(st1, st2, bands_f, 1, PAD)
    temporal(st2, st3, bands_f, 2, 0)

    def send_output(k):
        if k >= 3:
            wait_some(send_out.at[k - 3], st3, Z if k > 3 else Z - 1)
        send_group(k, st3, out_f, me, send_out.at[k], recv_out.at[k])

    for k in range(3):
        send_output(k)
    out_f[me] = st3[me]

    block = iota((C, 128), 1) >> 4
    last = jnp.zeros((C, 128), F32)
    packed = jnp.zeros((C, 128), F32)
    for layer, (state, back) in enumerate(((st0, back1), (st1, back2), (st2, back3))):
        e = 2**layer
        span = G + 2 * e
        acc_t[...] = jnp.zeros_like(acc_t)

        @pl.loop(0, GROUPS)
        def _(g):
            wide = state[pl.ds(g * G + PAD - e, span)].reshape(span * C, N)
            own = back[pl.ds(g * G + PAD, G)].reshape(G * C, N)
            acc_t[pl.ds(0, span * C)] += mm_nt(wide, own)

        for k in range(3):
            folded = fold(acc_t[pl.ds(0, span * C)], span, k * e)
            if layer * 3 + k < 8:
                packed = jnp.where(block == layer * 3 + k, folded, packed)
            else:
                last = jnp.where((block & 1) == 1, folded, last)
    packed_t = packed

    acc_s[...] = jnp.zeros_like(acc_s)

    @pl.loop(0, GROUPS)
    def _(k):
        wait_group(recv_grad.at[k], grad_f, k)
        g = lax.rem(q + Q - k, Q)
        rows = pl.ds(g * G, G)
        p = preact[rows].reshape(G * C, N)
        s = 1.0 / (1.0 + jnp.exp(-p))
        slope = grad_f[rows].reshape(G * C, N).astype(F32) * (s * (1.0 + p * (1.0 - s)))
        own = slope.astype(BF16)
        padded = pl.ds(g * G + 1, G)
        slopes[0, padded] = jnp.where(lane == N - 1, 0.0, pltpu.roll(slope, N - 1, 1)).astype(BF16).reshape(G, C, N)
        slopes[1, padded] = own.reshape(G, C, N)
        slopes[2, padded] = jnp.where(lane == 0, 0.0, pltpu.roll(slope, 1, 1)).astype(BF16).reshape(G, C, N)
        for b in range(3):
            acc_s[b] += mm_nt(xs[b, pl.ds(g * G, G + 2)].reshape((G + 2) * C, N), own)

    packed_s = jnp.zeros((C, 128), F32)
    for b in range(3):
        for a in range(3):
            folded = fold(acc_s[b], G + 2, a)
            if a * 3 + b < 8:
                packed_s = jnp.where(block == a * 3 + b, folded, packed_s)
            else:
                last = jnp.where((block & 1) == 0, folded, last)
    packed_l = jnp.zeros((4, 128), F32)
    for m in range(4):
        packed_l = jnp.where((block[:4] >> 1) == m, last[4 * m : 4 * m + 4], packed_l)
    for m in range(4):
        pack[m, :4] = packed_s[4 * m : 4 * m + 4]
        pack[m, 4:] = packed_l[m : m + 1]
        pack[m + 4, :4] = packed_t[4 * m : 4 * m + 4]
        pack[m + 4, 4:] = jnp.zeros((1, 128), F32)

    def to_columns(src_of, dst, index):
        for d in range(1, Q):
            other = lax.rem(q + d, Q)
            pltpu.make_async_remote_copy(
                src_ref=src_of(other), dst_ref=dst.at[q], send_sem=send_sem.at[index], recv_sem=recv_sem.at[index],
                device_id={"seq": other * Z + z}, device_id_type=MESH,
            ).start()

    def clip_gradient(g):
        total = jnp.zeros((C * G, N), F32)
        for b in range(3):
            total = total + mm(bands_v[b], slopes[b, pl.ds(g * G, G + 2)].reshape((G + 2) * C, N))
        grad_v[:, pl.ds(pl.multiple_of(g * G, G), G), :] = total.astype(BF16).reshape(C, G, N)

    to_columns(lambda other: pack.at[other], sum1, 3)
    sum1[q] = pack[q]
    send_output(3)

    @pl.loop(0, GROUPS // 2)
    def _(g):
        clip_gradient(g)

    wait_some(recv_sem.at[3], sum1, Q - 1)
    part1[...] = jnp.sum(sum1[...], axis=0)
    for d in range(1, Z):
        other = lax.rem(z + d, Z)
        pltpu.make_async_remote_copy(
            src_ref=part1, dst_ref=sum2.at[z], send_sem=send_sem.at[4], recv_sem=recv_sem.at[4],
            device_id={"seq": q * Z + other}, device_id_type=MESH,
        ).start()
    sum2[z] = part1[...]
    send_output(4)
    send_output(5)

    @pl.loop(GROUPS // 2, GROUPS)
    def _(g):
        clip_gradient(g)

    grad_store = pltpu.make_async_copy(grad_v, grad_hbm.at[0], local_sem.at[0])
    grad_store.start()
    send_output(6)

    wait_some(recv_sem.at[4], sum2, Z - 1)
    part2[...] = jnp.sum(sum2[...], axis=0)
    to_columns(lambda other: part2, sum3, 5)
    sum3[q] = part2[...]
    send_output(7)

    def output_rows(k):
        wait_group(recv_out.at[k], out_f, k)
        rows = pl.ds(pl.multiple_of(lax.rem(q + Q - k, Q) * G, G), G)
        out_v[:, rows, :] = mm(swap, out_f[rows].reshape(G * C, N)).astype(BF16).reshape(C, G, N)
        pltpu.make_async_copy(out_v.at[:, rows, :], out_hbm.at[0, :, rows, :], local_sem.at[1]).start()

    @pl.loop(0, GROUPS // 2)
    def _(k):
        output_rows(k)

    wait_some(recv_sem.at[5], sum3, Q - 1)
    for m in range(4):
        total[pl.ds(4 * m, 4)] = sum3[m, :4] * factor
        total[pl.ds(16 + 4 * m, 4)] = sum3[m + 4, :4] * factor
        total[pl.ds(32 + m, 1)] = sum3[m, 4:] * factor
    last = total[pl.ds(32, 4)]
    for tap in range(9):
        at = (128 - tap * C) % 128
        if tap < 8:
            sgrad_ref[tap // 3, tap % 3] = pltpu.roll(total[pl.ds(0, C)], at, 1)[:, :C] if at else total[pl.ds(0, C)][:, :C]
            tgrad_ref[tap // 3, tap % 3] = pltpu.roll(total[pl.ds(C, C)], at, 1)[:, :C] if at else total[pl.ds(C, C)][:, :C]
        else:
            for m in range(4):
                back_by = (128 - 32 * m) % 128
                sgrad_ref[2, 2, pl.ds(4 * m, 4)] = (pltpu.roll(last, back_by, 1) if back_by else last)[:, :C]
                tgrad_ref[2, 2, pl.ds(4 * m, 4)] = pltpu.roll(last, back_by - C if m else 128 - C, 1)[:, :C]

    @pl.loop(GROUPS // 2, GROUPS)
    def _(k):
        output_rows(k)

    wait_some(send_sem.at[0], cot_z, Z - 1)
    wait_all(send_sem.at[1], back0)
    wait_some(send_sem.at[2], back3, SEQ - Z)
    for k in range(5, Q):
        wait_some(send_act.at[k], act_f, Z)
        wait_some(send_out.at[k], st3, Z)
    wait_some(send_sem.at[3], sum1, Q - 1)
    wait_some(send_sem.at[4], sum2, Z - 1)
    wait_some(send_sem.at[5], sum3, Q - 1)
    grad_store.wait()
    pltpu.make_async_copy(out_v, out_hbm.at[0], local_sem.at[1]).wait()


def hand_over(out_in, grad_in, sgrad_in, tgrad_in, out_hbm, grad_hbm, sgrad_hbm, tgrad_hbm, *scratch):
    stages, load_sem, store_sem = scratch[:4], scratch[4], scratch[5]
    loads, stores = [], []
    pairs = zip((out_in, grad_in, sgrad_in, tgrad_in), stages, (out_hbm, grad_hbm, sgrad_hbm, tgrad_hbm))
    for source, stage, target in pairs:
        for part in range(HANDED if source.shape[0] == 1 else 1):
            at = (0, pl.ds(part * C // HANDED, C // HANDED)) if source.shape[0] == 1 else slice(None)
            loads.append(pltpu.make_async_copy(source.at[at], stage.at[at], load_sem.at[len(loads)]))
            stores.append(pltpu.make_async_copy(stage.at[at], target.at[at], store_sem.at[len(stores)]))
    for load in loads:
        load.start()
    for load, store in zip(loads, stores):
        load.wait()
        store.start()
    for store in stores:
        store.wait()


def body(clip_frames, cotangent, spatial_weight, temporal_weight):
    factor = 1.0 / math.sqrt(N * N * N)
    vmem = pl.BlockSpec(memory_space=pltpu.VMEM)
    anywhere = pl.BlockSpec(memory_space=pltpu.HBM)
    frame = pltpu.VMEM((N, C, N), BF16)
    padded = pltpu.VMEM((N + 2 * PAD, C, N), BF16)
    results = pl.pallas_call(
        functools.partial(kernel, factor),
        out_shape=(
            jax.ShapeDtypeStruct((1, C, N, N), BF16),
            jax.ShapeDtypeStruct((1, C, N, N), BF16),
            jax.ShapeDtypeStruct((3, 3, C, C), F32),
            jax.ShapeDtypeStruct((3, 3, C, C), F32),
        ),
        in_specs=[anywhere] * 4,
        out_specs=(anywhere, anywhere, vmem, vmem),
        scratch_shapes=[
            pltpu.VMEM((3, 3, C, C), BF16),
            pltpu.VMEM((3, 3, C, C), BF16),
            pltpu.VMEM((C, N, N), BF16),
            pltpu.VMEM((C, N, N), BF16),
            pltpu.VMEM((Q, Z, C, N), BF16),
            pltpu.VMEM((Z, Q, C, N), BF16),
            frame,
            pltpu.VMEM((3, N + 2, C, N), BF16),
            pltpu.VMEM((N, C, N), F32),
            pltpu.VMEM((3, G * C, (G + 2) * C), BF16),
            pltpu.VMEM((3, G * C, (G + 2) * C), BF16),
            pltpu.VMEM((3, G * C, (G + 8) * C), BF16),
            pltpu.VMEM((3, G * C, (G + 8) * C), BF16),
            padded, padded, padded, frame,
            padded, padded, padded, frame,
            frame,
            frame,
            pltpu.VMEM((3, N + 2, C, N), BF16),
            pltpu.VMEM(((G + 8) * C, G * C), F32),
            pltpu.VMEM((3, (G + 2) * C, G * C), F32),
            pltpu.VMEM((Q, PIECE, 128), F32),
            pltpu.VMEM((Q, PIECE, 128), F32),
            pltpu.VMEM((PIECE, 128), F32),
            pltpu.VMEM((Z, PIECE, 128), F32),
            pltpu.VMEM((PIECE, 128), F32),
            pltpu.VMEM((Q, PIECE, 128), F32),
            pltpu.VMEM((40, 128), F32),
            pltpu.VMEM((C, N, N), BF16),
            pltpu.VMEM((C, N, N), BF16),
            pltpu.SemaphoreType.DMA((4,)),
            pltpu.SemaphoreType.DMA((6,)),
            pltpu.SemaphoreType.DMA((6,)),
            pltpu.SemaphoreType.DMA((Q,)),
            pltpu.SemaphoreType.DMA((Q,)),
            pltpu.SemaphoreType.DMA((Q,)),
            pltpu.SemaphoreType.DMA((Q,)),
            pltpu.SemaphoreType.REGULAR,
        ],
        compiler_params=pltpu.CompilerParams(collective_id=0, has_side_effects=True, vmem_limit_bytes=VMEM_LIMIT),
    )(clip_frames, cotangent, spatial_weight, temporal_weight)
    return pl.pallas_call(
        hand_over,
        out_shape=tuple(jax.ShapeDtypeStruct(r.shape, r.dtype) for r in results),
        in_specs=[anywhere] * 4,
        out_specs=(anywhere,) * 4,
        scratch_shapes=[pltpu.VMEM(r.shape, r.dtype) for r in results] + [pltpu.SemaphoreType.DMA((2 * HANDED + 2,))] * 2,
        compiler_params=pltpu.CompilerParams(vmem_limit_bytes=VMEM_LIMIT),
    )(*results)


def solution(mesh):
    placed = (P(("dp", "seq"), None, None, None), P(("dp", "seq"), None, None, None), P(), P())
    return jax.shard_map(
        body,
        mesh=mesh,
        in_specs=placed,
        out_specs=(
            P(("dp", "seq"), None, None, None),
            P(("dp", "seq"), None, None, None),
            P("dp", None, None, None),
            P("dp", None, None, None),
        ),
        check_vma=False,
    )
```

```python
import functools
import math

import jax
import jax.numpy as jnp
from jax import lax
from jax.experimental import pallas as pl
from jax.experimental.pallas import tpu as pltpu
from jax.sharding import PartitionSpec as P

MESH = pl.DeviceIdType.MESH
F32 = jnp.float32
BF16 = jnp.bfloat16
C = 16
N = 128
SEQ = 128
Z = 16
Q = SEQ // Z
G = 16
GROUPS = N // G
PAD = 4
PIECES = 2 * Q
PIECE = 3
VMEM_LIMIT = 60 << 20
HANDED = 4


def iota(shape, axis):
    return lax.broadcasted_iota(jnp.int32, shape, axis)


def mm(a, b):
    return lax.dot_general(a, b, (((1,), (0,)), ((), ())), preferred_element_type=F32)


def mm_nt(a, b):
    return lax.dot_general(a, b, (((1,), (1,)), ((), ())), preferred_element_type=F32)


def one_hot(cond):
    return jnp.where(cond, 1.0, 0.0).astype(BF16)


def banded(weights, span, offsets, transposed, out_channel_major=False):
    cols = span * C
    i = iota((G * C, cols), 0)
    j = iota((G * C, cols), 1)
    si = iota((G * C, C), 0)
    sj = iota((G * C, C), 1)
    if out_channel_major:
        place = i & (G - 1)
        spread = one_hot((si >> 4) == sj)
    else:
        place = i >> 4
        spread = one_hot((si & (C - 1)) == sj)
    tile = one_hot(iota((C, cols), 0) == (iota((C, cols), 1) & (C - 1)))
    diff = (j >> 4) - place
    total = jnp.zeros((G * C, cols), F32)
    for weight, offset in zip(weights, offsets):
        rows = (mm if transposed else mm_nt)(spread, weight).astype(BF16)
        total = jnp.where(diff == offset, mm(rows, tile), total)
    return total.astype(BF16)


def fold(acc, span, offset):
    rows = span * C
    diff = (iota((rows, G * C), 0) >> 4) - (iota((rows, G * C), 1) >> 4)
    kept = jnp.where(diff == offset, acc, 0.0)
    total = jnp.sum(kept.reshape(span, C, G * C), axis=0)
    total = total[:, :128] + total[:, 128:]
    for step in (64, 32, 16):
        total = total + pltpu.roll(total, step, 1)
    return total


def kernel(
    factor,
    clip_hbm, cot_hbm, sw_hbm, tw_hbm,
    out_hbm, grad_hbm, sgrad_hbm, tgrad_hbm,
    sw_ref, tw_ref, sgrad_ref, tgrad_ref, clip_in, cot_in, cot_f, cot_z, act_f, xs, preact, bands_s, bands_v, bands_f, bands_b,
    back3, back2, back1, back0, st0, st1, st2, st3, grad_f, out_f, slopes,
    acc_t, acc_s, pack, sum1, part1, sum2, part2, sum3, total, out_v, grad_v,
    local_sem, send_sem, recv_sem, send_act, send_out, recv_grad, recv_out, ready,
):
    me = lax.axis_index("seq")
    q, z = me // Z, lax.rem(me, Z)

    cot_load = pltpu.make_async_copy(cot_hbm.at[0], cot_in, local_sem.at[0])
    cot_load.start()
    clip_load = pltpu.make_async_copy(clip_hbm.at[0], clip_in, local_sem.at[1])
    clip_load.start()
    sw_load = pltpu.make_async_copy(sw_hbm, sw_ref, local_sem.at[2])
    sw_load.start()
    tw_load = pltpu.make_async_copy(tw_hbm, tw_ref, local_sem.at[3])
    tw_load.start()

    barrier = pltpu.get_barrier_semaphore()
    for d in range(1, Q):
        pl.semaphore_signal(barrier, inc=1, device_id={"seq": lax.rem(q + d, Q) * Z + z}, device_id_type=MESH)
    for d in range(1, Z):
        pl.semaphore_signal(barrier, inc=1, device_id={"seq": q * Z + lax.rem(z + d, Z)}, device_id_type=MESH)

    def send_group(k, src, dst, at, sent, received):
        column = lax.rem(q + k, Q) * Z

        def send(i):
            j = 8 + lax.rem(i, 2) * (i + 1) // 2 - (1 - lax.rem(i, 2)) * (i // 2)
            t = column + lax.rem(z + j, Z)
            pltpu.make_async_remote_copy(
                src_ref=src.at[t], dst_ref=dst.at[at], send_sem=sent, recv_sem=received,
                device_id={"seq": t}, device_id_type=MESH,
            ).start()

        @pl.loop(0, Z if k else Z - 1)
        def _(i):
            send(i)

    def wait_some(sem, ref, count):
        part = ref.at[pl.ds(0, count)]
        pltpu.make_async_copy(part, part, sem).wait()

    def wait_all(sem, ref):
        wait_some(sem, ref, SEQ - 1)

    def wait_group(sem, ref, k):
        @pl.when(k == 0)
        def _():
            wait_some(sem, ref, Z - 1)

        @pl.when(k > 0)
        def _():
            wait_some(sem, ref, Z)

    i = iota((G * C, G * C), 0)
    j = iota((G * C, G * C), 1)
    swap = one_hot(((i & (C - 1)) == (j >> 4)) & ((i >> 4) == (j & (G - 1))))

    cot_load.wait()

    @pl.loop(0, GROUPS)
    def _(g):
        rows = pl.ds(pl.multiple_of(g * G, G), G)
        cot_f[g] = mm(swap, cot_in[:, rows, :].reshape(C * G, N)).astype(BF16).reshape(G, C, N)

    pl.semaphore_wait(barrier, Q - 1 + Z - 1)

    @pl.loop(1, Z)
    def _(d):
        other = lax.rem(z + d, Z)
        pltpu.make_async_remote_copy(
            src_ref=cot_f.at[:, other], dst_ref=cot_z.at[z], send_sem=send_sem.at[0], recv_sem=recv_sem.at[0],
            device_id={"seq": q * Z + other}, device_id_type=MESH,
        ).start()

    for d in range(1, Z):
        pl.semaphore_signal(ready, inc=1, device_id={"seq": q * Z + lax.rem(z + d, Z)}, device_id_type=MESH)
    cot_z[z] = cot_f[:, z]

    clip_load.wait()
    sw_load.wait()
    tw_load.wait()
    for b in range(3):
        bands_s[b] = banded([sw_ref[a, b] for a in range(3)], G + 2, range(3), False)
        xs[b, 0] = jnp.zeros((C, N), BF16)
        xs[b, N + 1] = jnp.zeros((C, N), BF16)
    lane = iota((G * C, N), 1)

    @pl.loop(0, GROUPS)
    def _(g):
        rows = pl.ds(pl.multiple_of(g * G, G), G)
        x = mm(swap, clip_in[:, rows, :].reshape(C * G, N))
        padded = pl.ds(g * G + 1, G)
        xs[0, padded] = jnp.where(lane == 0, 0.0, pltpu.roll(x, 1, 1)).astype(BF16).reshape(G, C, N)
        xs[1, padded] = x.astype(BF16).reshape(G, C, N)
        xs[2, padded] = jnp.where(lane == N - 1, 0.0, pltpu.roll(x, N - 1, 1)).astype(BF16).reshape(G, C, N)

    @pl.loop(0, GROUPS)
    def _(g):
        p = jnp.zeros((G * C, N), F32)
        for b in range(3):
            p = p + mm(bands_s[b], xs[b, pl.ds(g * G, G + 2)].reshape((G + 2) * C, N))
        rows = pl.ds(g * G, G)
        preact[rows] = p.reshape(G, C, N)
        act_f[rows] = (p / (1.0 + jnp.exp(-p))).astype(BF16).reshape(G, C, N)

    pl.semaphore_wait(ready, Z - 1)

    def send_activated(k):
        if k >= 3:
            wait_some(send_act.at[k - 3], act_f, Z if k > 3 else Z - 1)
        send_group(k, act_f, st0, me + PAD, send_act.at[k], recv_sem.at[1])

    for k in range(3):
        send_activated(k)
    st0[me + PAD] = act_f[me]

    zeros = jnp.zeros((PAD, C, N), BF16)
    for ref in (back3, back2, back1, st0, st1, st2):
        ref[pl.ds(0, PAD)] = zeros
        ref[pl.ds(N + PAD, PAD)] = zeros
    for layer in range(3):
        e = 2**layer
        span = G + 2 * e
        taps = [tw_ref[layer, k] for k in range(3)]
        bands_b[layer, :, pl.ds(0, span * C)] = banded(taps, span, [(2 - k) * e for k in range(3)], True)
        bands_f[layer, :, pl.ds(0, span * C)] = banded(taps, span, [k * e for k in range(3)], False)

    def temporal(src, dst, bands, layer, pad):
        e = 2**layer
        span = G + 2 * e

        @pl.loop(0, GROUPS)
        def _(g):
            own = src[pl.ds(g * G + PAD, G)].reshape(G * C, N).astype(F32)
            wide = src[pl.ds(g * G + PAD - e, span)].reshape(span * C, N)
            new = own + mm(bands[layer, :, pl.ds(0, span * C)], wide)
            dst[pl.ds(g * G + pad, G)] = new.astype(BF16).reshape(G, C, N)

    wait_some(recv_sem.at[0], cot_z, Z - 1)
    own_frames = pl.ds(q * Z + PAD, Z)
    for k in range(1, Q):
        other = lax.rem(q + k, Q)
        pltpu.make_async_remote_copy(
            src_ref=cot_z.at[:, other], dst_ref=back3.at[own_frames], send_sem=send_sem.at[2], recv_sem=recv_sem.at[2],
            device_id={"seq": other * Z + z}, device_id_type=MESH,
        ).start()
    back3[own_frames] = cot_z[:, q]
    for k in range(3, Q):
        send_activated(k)

    wait_some(recv_sem.at[2], back3, SEQ - Z)
    temporal(back3, back2, bands_b, 2, PAD)
    temporal(back2, back1, bands_b, 1, PAD)
    temporal(back1, back0, bands_b, 0, 0)
    for k in range(Q):
        send_group(k, back0, grad_f, me, send_sem.at[1], recv_grad.at[k])
    grad_f[me] = back0[me]
    for b in range(3):
        bands_v[b] = banded([sw_ref[a, b] for a in range(3)], G + 2, [2 - a for a in range(3)], True, True)
        slopes[b, 0] = jnp.zeros((C, N), BF16)
        slopes[b, N + 1] = jnp.zeros((C, N), BF16)

    wait_all(recv_sem.at[1], st0)
    temporal(st0, st1, bands_f, 0, PAD)
    temporal(st1, st2, bands_f, 1, PAD)
    temporal(st2, st3, bands_f, 2, 0)

    def send_output(k):
        if k >= 3:
            wait_some(send_out.at[k - 3], st3, Z if k > 3 else Z - 1)
        send_group(k, st3, out_f, me, send_out.at[k], recv_out.at[k])

    for k in range(2):
        send_output(k)
    out_f[me] = st3[me]

    block = iota((C, 128), 1) >> 4
    last = jnp.zeros((C, 128), F32)
    packed = jnp.zeros((C, 128), F32)
    for layer, (state, back) in enumerate(((st0, back1), (st1, back2), (st2, back3))):
        e = 2**layer
        span = G + 2 * e
        acc_t[...] = jnp.zeros_like(acc_t)

        @pl.loop(0, GROUPS)
        def _(g):
            wide = state[pl.ds(g * G + PAD - e, span)].reshape(span * C, N)
            own = back[pl.ds(g * G + PAD, G)].reshape(G * C, N)
            acc_t[pl.ds(0, span * C)] += mm_nt(wide, own)

        for k in range(3):
            folded = fold(acc_t[pl.ds(0, span * C)], span, k * e)
            if layer * 3 + k < 8:
                packed = jnp.where(block == layer * 3 + k, folded, packed)
            else:
                last = jnp.where((block & 1) == 1, folded, last)
    packed_t = packed

    acc_s[...] = jnp.zeros_like(acc_s)

    @pl.loop(0, GROUPS)
    def _(k):
        wait_group(recv_grad.at[k], grad_f, k)
        g = lax.rem(q + Q - k, Q)
        rows = pl.ds(g * G, G)
        p = preact[rows].reshape(G * C, N)
        s = 1.0 / (1.0 + jnp.exp(-p))
        slope = grad_f[rows].reshape(G * C, N).astype(F32) * (s * (1.0 + p * (1.0 - s)))
        own = slope.astype(BF16)
        padded = pl.ds(g * G + 1, G)
        slopes[0, padded] = jnp.where(lane == N - 1, 0.0, pltpu.roll(slope, N - 1, 1)).astype(BF16).reshape(G, C, N)
        slopes[1, padded] = own.reshape(G, C, N)
        slopes[2, padded] = jnp.where(lane == 0, 0.0, pltpu.roll(slope, 1, 1)).astype(BF16).reshape(G, C, N)
        for b in range(3):
            acc_s[b] += mm_nt(xs[b, pl.ds(g * G, G + 2)].reshape((G + 2) * C, N), own)

    packed_s = jnp.zeros((C, 128), F32)
    for b in range(3):
        for a in range(3):
            folded = fold(acc_s[b], G + 2, a)
            if a * 3 + b < 8:
                packed_s = jnp.where(block == a * 3 + b, folded, packed_s)
            else:
                last = jnp.where((block & 1) == 0, folded, last)
    packed_l = jnp.zeros((4, 128), F32)
    for m in range(4):
        packed_l = jnp.where((block[:4] >> 1) == m, last[4 * m : 4 * m + 4], packed_l)
    for m in range(PIECES // 2):
        pack[m, :2] = packed_s[2 * m : 2 * m + 2]
        pack[m + 8, :2] = packed_t[2 * m : 2 * m + 2]
        pack[m, 2:] = packed_l[m : m + 1] if m < 4 else jnp.zeros((1, 128), F32)
        pack[m + 8, 2:] = jnp.zeros((1, 128), F32)

    piece = q * 2 + lax.rem(z, 2)
    pair = z // 2

    def to_group(src_of, dst, index):
        @pl.loop(1, PIECES)
        def _(d):
            other = lax.rem(piece + d, PIECES)
            pltpu.make_async_remote_copy(
                src_ref=src_of(other), dst_ref=dst.at[piece], send_sem=send_sem.at[index], recv_sem=recv_sem.at[index],
                device_id={"seq": (other // 2) * Z + pair * 2 + lax.rem(other, 2)}, device_id_type=MESH,
            ).start()

    def clip_gradient(g):
        total = jnp.zeros((C * G, N), F32)
        for b in range(3):
            total = total + mm(bands_v[b], slopes[b, pl.ds(g * G, G + 2)].reshape((G + 2) * C, N))
        grad_v[:, pl.ds(pl.multiple_of(g * G, G), G), :] = total.astype(BF16).reshape(C, G, N)

    to_group(lambda other: pack.at[other], sum1, 3)
    sum1[piece] = pack[piece]
    send_output(2)
    send_output(3)

    @pl.loop(0, GROUPS // 2)
    def _(g):
        clip_gradient(g)

    wait_some(recv_sem.at[3], sum1, PIECES - 1)
    part1[...] = jnp.sum(sum1[...], axis=0)
    for d in range(1, Z // 2):
        other = lax.rem(z + 2 * d, Z)
        pltpu.make_async_remote_copy(
            src_ref=part1, dst_ref=sum2.at[pair], send_sem=send_sem.at[4], recv_sem=recv_sem.at[4],
            device_id={"seq": q * Z + other}, device_id_type=MESH,
        ).start()
    sum2[pair] = part1[...]
    send_output(4)
    send_output(5)

    @pl.loop(GROUPS // 2, GROUPS)
    def _(g):
        clip_gradient(g)

    grad_store = pltpu.make_async_copy(grad_v, grad_hbm.at[0], local_sem.at[0])
    grad_store.start()
    send_output(6)

    wait_some(recv_sem.at[4], sum2, Z // 2 - 1)
    part2[...] = jnp.sum(sum2[...], axis=0)
    to_group(lambda other: part2, sum3, 5)
    sum3[piece] = part2[...]
    send_output(7)

    def output_rows(k):
        wait_group(recv_out.at[k], out_f, k)
        rows = pl.ds(pl.multiple_of(lax.rem(q + Q - k, Q) * G, G), G)
        out_v[:, rows, :] = mm(swap, out_f[rows].reshape(G * C, N)).astype(BF16).reshape(C, G, N)
        pltpu.make_async_copy(out_v.at[:, rows, :], out_hbm.at[0, :, rows, :], local_sem.at[1]).start()

    @pl.loop(0, GROUPS - 1)
    def _(k):
        output_rows(k)

    wait_some(recv_sem.at[5], sum3, PIECES - 1)
    for m in range(PIECES):
        total[pl.ds(2 * m, 2)] = sum3[m, :2] * factor
    for m in range(4):
        total[pl.ds(32 + m, 1)] = sum3[m, 2:] * factor
    last = total[pl.ds(32, 4)]
    for tap in range(9):
        at = (128 - tap * C) % 128
        if tap < 8:
            sgrad_ref[tap // 3, tap % 3] = pltpu.roll(total[pl.ds(0, C)], at, 1)[:, :C] if at else total[pl.ds(0, C)][:, :C]
            tgrad_ref[tap // 3, tap % 3] = pltpu.roll(total[pl.ds(C, C)], at, 1)[:, :C] if at else total[pl.ds(C, C)][:, :C]
        else:
            for m in range(4):
                back_by = (128 - 32 * m) % 128
                sgrad_ref[2, 2, pl.ds(4 * m, 4)] = (pltpu.roll(last, back_by, 1) if back_by else last)[:, :C]
                tgrad_ref[2, 2, pl.ds(4 * m, 4)] = pltpu.roll(last, back_by - C if m else 128 - C, 1)[:, :C]

    small_stores = [
        pltpu.make_async_copy(sgrad_ref, sgrad_hbm, local_sem.at[2]),
        pltpu.make_async_copy(tgrad_ref, tgrad_hbm, local_sem.at[3]),
    ]
    for store in small_stores:
        store.start()

    output_rows(GROUPS - 1)

    wait_some(send_sem.at[0], cot_z, Z - 1)
    wait_all(send_sem.at[1], back0)
    wait_some(send_sem.at[2], back3, SEQ - Z)
    for k in range(5, Q):
        wait_some(send_act.at[k], act_f, Z)
        wait_some(send_out.at[k], st3, Z)
    wait_some(send_sem.at[3], sum1, PIECES - 1)
    wait_some(send_sem.at[4], sum2, Z // 2 - 1)
    wait_some(send_sem.at[5], sum3, PIECES - 1)
    for store in small_stores:
        store.wait()
    grad_store.wait()
    pltpu.make_async_copy(out_v, out_hbm.at[0], local_sem.at[1]).wait()


def hand_over(out_in, grad_in, sgrad_in, tgrad_in, out_hbm, grad_hbm, sgrad_hbm, tgrad_hbm, *scratch):
    stages, load_sem, store_sem = scratch[:4], scratch[4], scratch[5]
    loads, stores = [], []
    pairs = zip((out_in, grad_in, sgrad_in, tgrad_in), stages, (out_hbm, grad_hbm, sgrad_hbm, tgrad_hbm))
    for source, stage, target in pairs:
        for part in range(HANDED if source.shape[0] == 1 else 1):
            at = (0, pl.ds(part * C // HANDED, C // HANDED)) if source.shape[0] == 1 else slice(None)
            loads.append(pltpu.make_async_copy(source.at[at], stage.at[at], load_sem.at[len(loads)]))
            stores.append(pltpu.make_async_copy(stage.at[at], target.at[at], store_sem.at[len(stores)]))
    for load in loads:
        load.start()
    for load, store in zip(loads, stores):
        load.wait()
        store.start()
    for store in stores:
        store.wait()


def body(clip_frames, cotangent, spatial_weight, temporal_weight):
    factor = 1.0 / math.sqrt(N * N * N)
    anywhere = pl.BlockSpec(memory_space=pltpu.HBM)
    frame = pltpu.VMEM((N, C, N), BF16)
    padded = pltpu.VMEM((N + 2 * PAD, C, N), BF16)
    results = pl.pallas_call(
        functools.partial(kernel, factor),
        out_shape=(
            jax.ShapeDtypeStruct((1, C, N, N), BF16),
            jax.ShapeDtypeStruct((1, C, N, N), BF16),
            jax.ShapeDtypeStruct((3, 3, C, C), F32),
            jax.ShapeDtypeStruct((3, 3, C, C), F32),
        ),
        in_specs=[anywhere] * 4,
        out_specs=(anywhere,) * 4,
        scratch_shapes=[
            pltpu.VMEM((3, 3, C, C), BF16),
            pltpu.VMEM((3, 3, C, C), BF16),
            pltpu.VMEM((3, 3, C, C), F32),
            pltpu.VMEM((3, 3, C, C), F32),
            pltpu.VMEM((C, N, N), BF16),
            pltpu.VMEM((C, N, N), BF16),
            pltpu.VMEM((Q, Z, C, N), BF16),
            pltpu.VMEM((Z, Q, C, N), BF16),
            frame,
            pltpu.VMEM((3, N + 2, C, N), BF16),
            pltpu.VMEM((N, C, N), F32),
            pltpu.VMEM((3, G * C, (G + 2) * C), BF16),
            pltpu.VMEM((3, G * C, (G + 2) * C), BF16),
            pltpu.VMEM((3, G * C, (G + 8) * C), BF16),
            pltpu.VMEM((3, G * C, (G + 8) * C), BF16),
            padded, padded, padded, frame,
            padded, padded, padded, frame,
            frame,
            frame,
            pltpu.VMEM((3, N + 2, C, N), BF16),
            pltpu.VMEM(((G + 8) * C, G * C), F32),
            pltpu.VMEM((3, (G + 2) * C, G * C), F32),
            pltpu.VMEM((PIECES, PIECE, 128), F32),
            pltpu.VMEM((PIECES, PIECE, 128), F32),
            pltpu.VMEM((PIECE, 128), F32),
            pltpu.VMEM((Z // 2, PIECE, 128), F32),
            pltpu.VMEM((PIECE, 128), F32),
            pltpu.VMEM((PIECES, PIECE, 128), F32),
            pltpu.VMEM((40, 128), F32),
            pltpu.VMEM((C, N, N), BF16),
            pltpu.VMEM((C, N, N), BF16),
            pltpu.SemaphoreType.DMA((4,)),
            pltpu.SemaphoreType.DMA((6,)),
            pltpu.SemaphoreType.DMA((6,)),
            pltpu.SemaphoreType.DMA((Q,)),
            pltpu.SemaphoreType.DMA((Q,)),
            pltpu.SemaphoreType.DMA((Q,)),
            pltpu.SemaphoreType.DMA((Q,)),
            pltpu.SemaphoreType.REGULAR,
        ],
        compiler_params=pltpu.CompilerParams(collective_id=0, has_side_effects=True, vmem_limit_bytes=VMEM_LIMIT),
    )(clip_frames, cotangent, spatial_weight, temporal_weight)
    return pl.pallas_call(
        hand_over,
        out_shape=tuple(jax.ShapeDtypeStruct(r.shape, r.dtype) for r in results),
        in_specs=[anywhere] * 4,
        out_specs=(anywhere,) * 4,
        scratch_shapes=[pltpu.VMEM(r.shape, r.dtype) for r in results] + [pltpu.SemaphoreType.DMA((2 * HANDED + 2,))] * 2,
        compiler_params=pltpu.CompilerParams(vmem_limit_bytes=VMEM_LIMIT),
    )(*results)


def solution(mesh):
    placed = (P(("dp", "seq"), None, None, None), P(("dp", "seq"), None, None, None), P(), P())
    return jax.shard_map(
        body,
        mesh=mesh,
        in_specs=placed,
        out_specs=(
            P(("dp", "seq"), None, None, None),
            P(("dp", "seq"), None, None, None),
            P("dp", None, None, None),
            P("dp", None, None, None),
        ),
        check_vma=False,
    )
```

```python
import functools
import math

import jax
import jax.numpy as jnp
from jax import lax
from jax.experimental import pallas as pl
from jax.experimental.pallas import tpu as pltpu
from jax.sharding import PartitionSpec as P

MESH = pl.DeviceIdType.MESH
F32 = jnp.float32
BF16 = jnp.bfloat16
C = 16
N = 128
SEQ = 128
Z = 16
Q = SEQ // Z
G = 16
GROUPS = N // G
PAD = 4
PIECES = 2 * Q
PIECE = 3
VMEM_LIMIT = 60 << 20
HANDED = 4


def iota(shape, axis):
    return lax.broadcasted_iota(jnp.int32, shape, axis)


def mm(a, b):
    return lax.dot_general(a, b, (((1,), (0,)), ((), ())), preferred_element_type=F32)


def mm_nt(a, b):
    return lax.dot_general(a, b, (((1,), (1,)), ((), ())), preferred_element_type=F32)


def one_hot(cond):
    return jnp.where(cond, 1.0, 0.0).astype(BF16)


def banded(weights, span, offsets, transposed, out_channel_major=False):
    cols = span * C
    i = iota((G * C, cols), 0)
    j = iota((G * C, cols), 1)
    si = iota((G * C, C), 0)
    sj = iota((G * C, C), 1)
    if out_channel_major:
        place = i & (G - 1)
        spread = one_hot((si >> 4) == sj)
    else:
        place = i >> 4
        spread = one_hot((si & (C - 1)) == sj)
    tile = one_hot(iota((C, cols), 0) == (iota((C, cols), 1) & (C - 1)))
    diff = (j >> 4) - place
    total = jnp.zeros((G * C, cols), F32)
    for weight, offset in zip(weights, offsets):
        rows = (mm if transposed else mm_nt)(spread, weight).astype(BF16)
        total = jnp.where(diff == offset, mm(rows, tile), total)
    return total.astype(BF16)


def fold(acc, span, offset):
    rows = span * C
    diff = (iota((rows, G * C), 0) >> 4) - (iota((rows, G * C), 1) >> 4)
    kept = jnp.where(diff == offset, acc, 0.0)
    total = jnp.sum(kept.reshape(span, C, G * C), axis=0)
    total = total[:, :128] + total[:, 128:]
    for step in (64, 32, 16):
        total = total + pltpu.roll(total, step, 1)
    return total


def kernel(
    factor,
    clip_hbm, cot_hbm, sw_hbm, tw_hbm,
    out_hbm, grad_hbm, sgrad_hbm, tgrad_hbm,
    sw_ref, tw_ref, sgrad_ref, tgrad_ref, clip_in, cot_in, cot_f, cot_z, act_f, xs, preact, bands_s, bands_v, bands_f, bands_b,
    back3, back2, back1, back0, st0, st1, st2, st3, grad_f, out_f, slopes,
    acc_t, acc_s, pack, sum1, part1, sum2, part2, sum3, total, out_v, grad_v,
    local_sem, send_sem, recv_sem, send_act, send_out, recv_grad, recv_out, ready,
):
    me = lax.axis_index("seq")
    q, z = me // Z, lax.rem(me, Z)

    cot_load = pltpu.make_async_copy(cot_hbm.at[0], cot_in, local_sem.at[0])
    cot_load.start()
    clip_load = pltpu.make_async_copy(clip_hbm.at[0], clip_in, local_sem.at[1])
    clip_load.start()
    sw_load = pltpu.make_async_copy(sw_hbm, sw_ref, local_sem.at[2])
    sw_load.start()
    tw_load = pltpu.make_async_copy(tw_hbm, tw_ref, local_sem.at[3])
    tw_load.start()

    barrier = pltpu.get_barrier_semaphore()
    for d in range(1, Q):
        pl.semaphore_signal(barrier, inc=1, device_id={"seq": lax.rem(q + d, Q) * Z + z}, device_id_type=MESH)
    for d in range(1, Z):
        pl.semaphore_signal(barrier, inc=1, device_id={"seq": q * Z + lax.rem(z + d, Z)}, device_id_type=MESH)

    def send_group(k, src, dst, at, sent, received):
        column = lax.rem(q + k, Q) * Z

        def send(i):
            j = 8 + lax.rem(i, 2) * (i + 1) // 2 - (1 - lax.rem(i, 2)) * (i // 2)
            t = column + lax.rem(z + j, Z)
            pltpu.make_async_remote_copy(
                src_ref=src.at[t], dst_ref=dst.at[at], send_sem=sent, recv_sem=received,
                device_id={"seq": t}, device_id_type=MESH,
            ).start()

        @pl.loop(0, Z if k else Z - 1)
        def _(i):
            send(i)

    def wait_some(sem, ref, count):
        part = ref.at[pl.ds(0, count)]
        pltpu.make_async_copy(part, part, sem).wait()

    def wait_all(sem, ref):
        wait_some(sem, ref, SEQ - 1)

    def wait_group(sem, ref, k):
        @pl.when(k == 0)
        def _():
            wait_some(sem, ref, Z - 1)

        @pl.when(k > 0)
        def _():
            wait_some(sem, ref, Z)

    i = iota((G * C, G * C), 0)
    j = iota((G * C, G * C), 1)
    swap = one_hot(((i & (C - 1)) == (j >> 4)) & ((i >> 4) == (j & (G - 1))))

    cot_load.wait()

    @pl.loop(0, GROUPS)
    def _(g):
        rows = pl.ds(pl.multiple_of(g * G, G), G)
        cot_f[g] = mm(swap, cot_in[:, rows, :].reshape(C * G, N)).astype(BF16).reshape(G, C, N)

    pl.semaphore_wait(barrier, Q - 1 + Z - 1)

    @pl.loop(1, Z)
    def _(d):
        other = lax.rem(z + d, Z)
        pltpu.make_async_remote_copy(
            src_ref=cot_f.at[:, other], dst_ref=cot_z.at[z], send_sem=send_sem.at[0], recv_sem=recv_sem.at[0],
            device_id={"seq": q * Z + other}, device_id_type=MESH,
        ).start()

    for d in range(1, Z):
        pl.semaphore_signal(ready, inc=1, device_id={"seq": q * Z + lax.rem(z + d, Z)}, device_id_type=MESH)
    cot_z[z] = cot_f[:, z]

    clip_load.wait()
    sw_load.wait()
    tw_load.wait()
    for b in range(3):
        bands_s[b] = banded([sw_ref[a, b] for a in range(3)], G + 2, range(3), False)
        xs[b, 0] = jnp.zeros((C, N), BF16)
        xs[b, N + 1] = jnp.zeros((C, N), BF16)
    lane = iota((G * C, N), 1)

    @pl.loop(0, GROUPS)
    def _(g):
        rows = pl.ds(pl.multiple_of(g * G, G), G)
        x = mm(swap, clip_in[:, rows, :].reshape(C * G, N))
        padded = pl.ds(g * G + 1, G)
        xs[0, padded] = jnp.where(lane == 0, 0.0, pltpu.roll(x, 1, 1)).astype(BF16).reshape(G, C, N)
        xs[1, padded] = x.astype(BF16).reshape(G, C, N)
        xs[2, padded] = jnp.where(lane == N - 1, 0.0, pltpu.roll(x, N - 1, 1)).astype(BF16).reshape(G, C, N)

    @pl.loop(0, GROUPS)
    def _(g):
        p = jnp.zeros((G * C, N), F32)
        for b in range(3):
            p = p + mm(bands_s[b], xs[b, pl.ds(g * G, G + 2)].reshape((G + 2) * C, N))
        rows = pl.ds(g * G, G)
        preact[rows] = p.reshape(G, C, N)
        act_f[rows] = (p / (1.0 + jnp.exp(-p))).astype(BF16).reshape(G, C, N)

    pl.semaphore_wait(ready, Z - 1)

    def send_activated(k):
        if k >= 3:
            wait_some(send_act.at[k - 3], act_f, Z if k > 3 else Z - 1)
        send_group(k, act_f, st0, me + PAD, send_act.at[k], recv_sem.at[1])

    for k in range(3):
        send_activated(k)
    st0[me + PAD] = act_f[me]

    zeros = jnp.zeros((PAD, C, N), BF16)
    for ref in (back3, back2, back1, st0, st1, st2):
        ref[pl.ds(0, PAD)] = zeros
        ref[pl.ds(N + PAD, PAD)] = zeros
    for layer in range(3):
        e = 2**layer
        span = G + 2 * e
        taps = [tw_ref[layer, k] for k in range(3)]
        bands_b[layer, :, pl.ds(0, span * C)] = banded(taps, span, [(2 - k) * e for k in range(3)], True)
        bands_f[layer, :, pl.ds(0, span * C)] = banded(taps, span, [k * e for k in range(3)], False)

    def temporal(src, dst, bands, layer, pad):
        e = 2**layer
        span = G + 2 * e

        @pl.loop(0, GROUPS)
        def _(g):
            own = src[pl.ds(g * G + PAD, G)].reshape(G * C, N).astype(F32)
            wide = src[pl.ds(g * G + PAD - e, span)].reshape(span * C, N)
            new = own + mm(bands[layer, :, pl.ds(0, span * C)], wide)
            dst[pl.ds(g * G + pad, G)] = new.astype(BF16).reshape(G, C, N)

    wait_some(recv_sem.at[0], cot_z, Z - 1)
    own_frames = pl.ds(q * Z + PAD, Z)
    for k in range(1, Q):
        other = lax.rem(q + k, Q)
        pltpu.make_async_remote_copy(
            src_ref=cot_z.at[:, other], dst_ref=back3.at[own_frames], send_sem=send_sem.at[2], recv_sem=recv_sem.at[2],
            device_id={"seq": other * Z + z}, device_id_type=MESH,
        ).start()
    back3[own_frames] = cot_z[:, q]
    for k in range(3, Q):
        send_activated(k)

    wait_some(recv_sem.at[2], back3, SEQ - Z)
    temporal(back3, back2, bands_b, 2, PAD)
    temporal(back2, back1, bands_b, 1, PAD)
    temporal(back1, back0, bands_b, 0, 0)
    for k in range(Q):
        send_group(k, back0, grad_f, me, send_sem.at[1], recv_grad.at[k])
    grad_f[me] = back0[me]
    for b in range(3):
        bands_v[b] = banded([sw_ref[a, b] for a in range(3)], G + 2, [2 - a for a in range(3)], True, True)
        slopes[b, 0] = jnp.zeros((C, N), BF16)
        slopes[b, N + 1] = jnp.zeros((C, N), BF16)

    wait_all(recv_sem.at[1], st0)
    temporal(st0, st1, bands_f, 0, PAD)
    temporal(st1, st2, bands_f, 1, PAD)
    temporal(st2, st3, bands_f, 2, 0)

    def send_output(k):
        if k >= 3:
            wait_some(send_out.at[k - 3], st3, Z if k > 3 else Z - 1)
        send_group(k, st3, out_f, me, send_out.at[k], recv_out.at[k])

    for k in range(2):
        send_output(k)
    out_f[me] = st3[me]

    block = iota((C, 128), 1) >> 4
    last = jnp.zeros((C, 128), F32)
    packed = jnp.zeros((C, 128), F32)
    for layer, (state, back) in enumerate(((st0, back1), (st1, back2), (st2, back3))):
        e = 2**layer
        span = G + 2 * e
        acc_t[...] = jnp.zeros_like(acc_t)

        @pl.loop(0, GROUPS)
        def _(g):
            wide = state[pl.ds(g * G + PAD - e, span)].reshape(span * C, N)
            own = back[pl.ds(g * G + PAD, G)].reshape(G * C, N)
            acc_t[pl.ds(0, span * C)] += mm_nt(wide, own)

        for k in range(3):
            folded = fold(acc_t[pl.ds(0, span * C)], span, k * e)
            if layer * 3 + k < 8:
                packed = jnp.where(block == layer * 3 + k, folded, packed)
            else:
                last = jnp.where((block & 1) == 1, folded, last)
    packed_t = packed

    acc_s[...] = jnp.zeros_like(acc_s)

    @pl.loop(0, GROUPS)
    def _(k):
        wait_group(recv_grad.at[k], grad_f, k)
        g = lax.rem(q + Q - k, Q)
        rows = pl.ds(g * G, G)
        p = preact[rows].reshape(G * C, N)
        s = 1.0 / (1.0 + jnp.exp(-p))
        slope = grad_f[rows].reshape(G * C, N).astype(F32) * (s * (1.0 + p * (1.0 - s)))
        own = slope.astype(BF16)
        padded = pl.ds(g * G + 1, G)
        slopes[0, padded] = jnp.where(lane == N - 1, 0.0, pltpu.roll(slope, N - 1, 1)).astype(BF16).reshape(G, C, N)
        slopes[1, padded] = own.reshape(G, C, N)
        slopes[2, padded] = jnp.where(lane == 0, 0.0, pltpu.roll(slope, 1, 1)).astype(BF16).reshape(G, C, N)
        for b in range(3):
            acc_s[b] += mm_nt(xs[b, pl.ds(g * G, G + 2)].reshape((G + 2) * C, N), own)

    packed_s = jnp.zeros((C, 128), F32)
    for b in range(3):
        for a in range(3):
            folded = fold(acc_s[b], G + 2, a)
            if a * 3 + b < 8:
                packed_s = jnp.where(block == a * 3 + b, folded, packed_s)
            else:
                last = jnp.where((block & 1) == 0, folded, last)
    packed_l = jnp.zeros((4, 128), F32)
    for m in range(4):
        packed_l = jnp.where((block[:4] >> 1) == m, last[4 * m : 4 * m + 4], packed_l)
    for m in range(PIECES // 2):
        pack[m, :2] = packed_s[2 * m : 2 * m + 2]
        pack[m + 8, :2] = packed_t[2 * m : 2 * m + 2]
        pack[m, 2:] = packed_l[m : m + 1] if m < 4 else jnp.zeros((1, 128), F32)
        pack[m + 8, 2:] = jnp.zeros((1, 128), F32)

    piece = q * 2 + lax.rem(z, 2)
    pair = z // 2

    def to_group(src_of, dst, index):
        @pl.loop(1, PIECES)
        def _(d):
            other = lax.rem(piece + d, PIECES)
            pltpu.make_async_remote_copy(
                src_ref=src_of(other), dst_ref=dst.at[piece], send_sem=send_sem.at[index], recv_sem=recv_sem.at[index],
                device_id={"seq": (other // 2) * Z + pair * 2 + lax.rem(other, 2)}, device_id_type=MESH,
            ).start()

    def clip_gradient(g):
        total = jnp.zeros((C * G, N), F32)
        for b in range(3):
            total = total + mm(bands_v[b], slopes[b, pl.ds(g * G, G + 2)].reshape((G + 2) * C, N))
        grad_v[:, pl.ds(pl.multiple_of(g * G, G), G), :] = total.astype(BF16).reshape(C, G, N)

    to_group(lambda other: pack.at[other], sum1, 3)
    sum1[piece] = pack[piece]
    send_output(2)
    send_output(3)

    @pl.loop(0, GROUPS // 2)
    def _(g):
        clip_gradient(g)

    wait_some(recv_sem.at[3], sum1, PIECES - 1)
    part1[...] = jnp.sum(sum1[...], axis=0)
    for d in range(1, Z // 2):
        other = lax.rem(z + 2 * d, Z)
        pltpu.make_async_remote_copy(
            src_ref=part1, dst_ref=sum2.at[pair], send_sem=send_sem.at[4], recv_sem=recv_sem.at[4],
            device_id={"seq": q * Z + other}, device_id_type=MESH,
        ).start()
    sum2[pair] = part1[...]
    send_output(4)
    send_output(5)

    @pl.loop(GROUPS // 2, GROUPS)
    def _(g):
        clip_gradient(g)

    grad_store = pltpu.make_async_copy(grad_v, grad_hbm.at[0], local_sem.at[0])
    grad_store.start()
    send_output(6)
    send_output(7)

    wait_some(recv_sem.at[4], sum2, Z // 2 - 1)
    part2[...] = jnp.sum(sum2[...], axis=0)
    to_group(lambda other: part2, sum3, 5)
    sum3[piece] = part2[...]

    def output_rows(k):
        wait_group(recv_out.at[k], out_f, k)
        rows = pl.ds(pl.multiple_of(lax.rem(q + Q - k, Q) * G, G), G)
        out_v[:, rows, :] = mm(swap, out_f[rows].reshape(G * C, N)).astype(BF16).reshape(C, G, N)
        pltpu.make_async_copy(out_v.at[:, rows, :], out_hbm.at[0, :, rows, :], local_sem.at[1]).start()

    @pl.loop(0, GROUPS - 1)
    def _(k):
        output_rows(k)

    wait_some(recv_sem.at[5], sum3, PIECES - 1)
    for m in range(PIECES):
        total[pl.ds(2 * m, 2)] = sum3[m, :2] * factor
    for m in range(4):
        total[pl.ds(32 + m, 1)] = sum3[m, 2:] * factor
    last = total[pl.ds(32, 4)]
    for tap in range(9):
        at = (128 - tap * C) % 128
        if tap < 8:
            sgrad_ref[tap // 3, tap % 3] = pltpu.roll(total[pl.ds(0, C)], at, 1)[:, :C] if at else total[pl.ds(0, C)][:, :C]
            tgrad_ref[tap // 3, tap % 3] = pltpu.roll(total[pl.ds(C, C)], at, 1)[:, :C] if at else total[pl.ds(C, C)][:, :C]
        else:
            for m in range(4):
                back_by = (128 - 32 * m) % 128
                sgrad_ref[2, 2, pl.ds(4 * m, 4)] = (pltpu.roll(last, back_by, 1) if back_by else last)[:, :C]
                tgrad_ref[2, 2, pl.ds(4 * m, 4)] = pltpu.roll(last, back_by - C if m else 128 - C, 1)[:, :C]

    small_stores = [
        pltpu.make_async_copy(sgrad_ref, sgrad_hbm, local_sem.at[2]),
        pltpu.make_async_copy(tgrad_ref, tgrad_hbm, local_sem.at[3]),
    ]
    for store in small_stores:
        store.start()

    output_rows(GROUPS - 1)

    wait_some(send_sem.at[0], cot_z, Z - 1)
    wait_all(send_sem.at[1], back0)
    wait_some(send_sem.at[2], back3, SEQ - Z)
    for k in range(5, Q):
        wait_some(send_act.at[k], act_f, Z)
        wait_some(send_out.at[k], st3, Z)
    wait_some(send_sem.at[3], sum1, PIECES - 1)
    wait_some(send_sem.at[4], sum2, Z // 2 - 1)
    wait_some(send_sem.at[5], sum3, PIECES - 1)
    for store in small_stores:
        store.wait()
    grad_store.wait()
    pltpu.make_async_copy(out_v, out_hbm.at[0], local_sem.at[1]).wait()


def hand_over(out_in, grad_in, sgrad_in, tgrad_in, out_hbm, grad_hbm, sgrad_hbm, tgrad_hbm, *scratch):
    stages, load_sem, store_sem = scratch[:4], scratch[4], scratch[5]
    loads, stores = [], []
    pairs = zip((out_in, grad_in, sgrad_in, tgrad_in), stages, (out_hbm, grad_hbm, sgrad_hbm, tgrad_hbm))
    for source, stage, target in pairs:
        for part in range(HANDED if source.shape[0] == 1 else 1):
            at = (0, pl.ds(part * C // HANDED, C // HANDED)) if source.shape[0] == 1 else slice(None)
            loads.append(pltpu.make_async_copy(source.at[at], stage.at[at], load_sem.at[len(loads)]))
            stores.append(pltpu.make_async_copy(stage.at[at], target.at[at], store_sem.at[len(stores)]))
    for load in loads:
        load.start()
    for load, store in zip(loads, stores):
        load.wait()
        store.start()
    for store in stores:
        store.wait()


def body(clip_frames, cotangent, spatial_weight, temporal_weight):
    factor = 1.0 / math.sqrt(N * N * N)
    anywhere = pl.BlockSpec(memory_space=pltpu.HBM)
    frame = pltpu.VMEM((N, C, N), BF16)
    padded = pltpu.VMEM((N + 2 * PAD, C, N), BF16)
    results = pl.pallas_call(
        functools.partial(kernel, factor),
        out_shape=(
            jax.ShapeDtypeStruct((1, C, N, N), BF16),
            jax.ShapeDtypeStruct((1, C, N, N), BF16),
            jax.ShapeDtypeStruct((3, 3, C, C), F32),
            jax.ShapeDtypeStruct((3, 3, C, C), F32),
        ),
        in_specs=[anywhere] * 4,
        out_specs=(anywhere,) * 4,
        scratch_shapes=[
            pltpu.VMEM((3, 3, C, C), BF16),
            pltpu.VMEM((3, 3, C, C), BF16),
            pltpu.VMEM((3, 3, C, C), F32),
            pltpu.VMEM((3, 3, C, C), F32),
            pltpu.VMEM((C, N, N), BF16),
            pltpu.VMEM((C, N, N), BF16),
            pltpu.VMEM((Q, Z, C, N), BF16),
            pltpu.VMEM((Z, Q, C, N), BF16),
            frame,
            pltpu.VMEM((3, N + 2, C, N), BF16),
            pltpu.VMEM((N, C, N), F32),
            pltpu.VMEM((3, G * C, (G + 2) * C), BF16),
            pltpu.VMEM((3, G * C, (G + 2) * C), BF16),
            pltpu.VMEM((3, G * C, (G + 8) * C), BF16),
            pltpu.VMEM((3, G * C, (G + 8) * C), BF16),
            padded, padded, padded, frame,
            padded, padded, padded, frame,
            frame,
            frame,
            pltpu.VMEM((3, N + 2, C, N), BF16),
            pltpu.VMEM(((G + 8) * C, G * C), F32),
            pltpu.VMEM((3, (G + 2) * C, G * C), F32),
            pltpu.VMEM((PIECES, PIECE, 128), F32),
            pltpu.VMEM((PIECES, PIECE, 128), F32),
            pltpu.VMEM((PIECE, 128), F32),
            pltpu.VMEM((Z // 2, PIECE, 128), F32),
            pltpu.VMEM((PIECE, 128), F32),
            pltpu.VMEM((PIECES, PIECE, 128), F32),
            pltpu.VMEM((40, 128), F32),
            pltpu.VMEM((C, N, N), BF16),
            pltpu.VMEM((C, N, N), BF16),
            pltpu.SemaphoreType.DMA((4,)),
            pltpu.SemaphoreType.DMA((6,)),
            pltpu.SemaphoreType.DMA((6,)),
            pltpu.SemaphoreType.DMA((Q,)),
            pltpu.SemaphoreType.DMA((Q,)),
            pltpu.SemaphoreType.DMA((Q,)),
            pltpu.SemaphoreType.DMA((Q,)),
            pltpu.SemaphoreType.REGULAR,
        ],
        compiler_params=pltpu.CompilerParams(collective_id=0, has_side_effects=True, vmem_limit_bytes=VMEM_LIMIT),
    )(clip_frames, cotangent, spatial_weight, temporal_weight)
    return pl.pallas_call(
        hand_over,
        out_shape=tuple(jax.ShapeDtypeStruct(r.shape, r.dtype) for r in results),
        in_specs=[anywhere] * 4,
        out_specs=(anywhere,) * 4,
        scratch_shapes=[pltpu.VMEM(r.shape, r.dtype) for r in results] + [pltpu.SemaphoreType.DMA((2 * HANDED + 2,))] * 2,
        compiler_params=pltpu.CompilerParams(vmem_limit_bytes=VMEM_LIMIT),
    )(*results)


def solution(mesh):
    placed = (P(("dp", "seq"), None, None, None), P(("dp", "seq"), None, None, None), P(), P())
    return jax.shard_map(
        body,
        mesh=mesh,
        in_specs=placed,
        out_specs=(
            P(("dp", "seq"), None, None, None),
            P(("dp", "seq"), None, None, None),
            P("dp", None, None, None),
            P("dp", None, None, None),
        ),
        check_vma=False,
    )
```

```python
import functools
import math

import jax
import jax.numpy as jnp
from jax import lax
from jax.experimental import pallas as pl
from jax.experimental.pallas import tpu as pltpu
from jax.sharding import PartitionSpec as P

MESH = pl.DeviceIdType.MESH
F32 = jnp.float32
BF16 = jnp.bfloat16
C = 16
N = 128
SEQ = 128
Z = 16
Q = SEQ // Z
G = 16
GROUPS = N // G
PAD = 4
PIECES = 2 * Q
PIECE = 3
VMEM_LIMIT = 60 << 20
HANDED = 1


def iota(shape, axis):
    return lax.broadcasted_iota(jnp.int32, shape, axis)


def mm(a, b):
    return lax.dot_general(a, b, (((1,), (0,)), ((), ())), preferred_element_type=F32)


def mm_nt(a, b):
    return lax.dot_general(a, b, (((1,), (1,)), ((), ())), preferred_element_type=F32)


def one_hot(cond):
    return jnp.where(cond, 1.0, 0.0).astype(BF16)


def banded(weights, span, offsets, transposed, out_channel_major=False):
    cols = span * C
    i = iota((G * C, cols), 0)
    j = iota((G * C, cols), 1)
    si = iota((G * C, C), 0)
    sj = iota((G * C, C), 1)
    if out_channel_major:
        place = i & (G - 1)
        spread = one_hot((si >> 4) == sj)
    else:
        place = i >> 4
        spread = one_hot((si & (C - 1)) == sj)
    tile = one_hot(iota((C, cols), 0) == (iota((C, cols), 1) & (C - 1)))
    diff = (j >> 4) - place
    total = jnp.zeros((G * C, cols), F32)
    for weight, offset in zip(weights, offsets):
        rows = (mm if transposed else mm_nt)(spread, weight).astype(BF16)
        total = jnp.where(diff == offset, mm(rows, tile), total)
    return total.astype(BF16)


def fold(acc, span, offset):
    rows = span * C
    diff = (iota((rows, G * C), 0) >> 4) - (iota((rows, G * C), 1) >> 4)
    kept = jnp.where(diff == offset, acc, 0.0)
    total = jnp.sum(kept.reshape(span, C, G * C), axis=0)
    total = total[:, :128] + total[:, 128:]
    for step in (64, 32, 16):
        total = total + pltpu.roll(total, step, 1)
    return total


def kernel(
    factor,
    clip_hbm, cot_hbm, sw_hbm, tw_hbm,
    out_hbm, grad_hbm, sgrad_hbm, tgrad_hbm,
    sw_ref, tw_ref, sgrad_ref, tgrad_ref, clip_in, cot_in, cot_f, cot_z, act_f, xs, preact, bands_s, bands_v, bands_f, bands_b,
    back3, back2, back1, back0, st0, st1, st2, st3, grad_f, out_f, slopes,
    acc_t, acc_s, pack, sum1, part1, sum2, part2, sum3, total, out_v, grad_v,
    local_sem, send_sem, recv_sem, send_act, send_out, recv_grad, recv_out, ready,
):
    me = lax.axis_index("seq")
    q, z = me // Z, lax.rem(me, Z)

    cot_load = pltpu.make_async_copy(cot_hbm.at[0], cot_in, local_sem.at[0])
    cot_load.start()
    clip_load = pltpu.make_async_copy(clip_hbm.at[0], clip_in, local_sem.at[1])
    clip_load.start()
    sw_load = pltpu.make_async_copy(sw_hbm, sw_ref, local_sem.at[2])
    sw_load.start()
    tw_load = pltpu.make_async_copy(tw_hbm, tw_ref, local_sem.at[3])
    tw_load.start()

    barrier = pltpu.get_barrier_semaphore()
    for d in range(1, Q):
        pl.semaphore_signal(barrier, inc=1, device_id={"seq": lax.rem(q + d, Q) * Z + z}, device_id_type=MESH)
    for d in range(1, Z):
        pl.semaphore_signal(barrier, inc=1, device_id={"seq": q * Z + lax.rem(z + d, Z)}, device_id_type=MESH)

    def send_group(k, src, dst, at, sent, received):
        column = lax.rem(q + k, Q) * Z

        def send(i):
            j = 8 + lax.rem(i, 2) * (i + 1) // 2 - (1 - lax.rem(i, 2)) * (i // 2)
            t = column + lax.rem(z + j, Z)
            pltpu.make_async_remote_copy(
                src_ref=src.at[t], dst_ref=dst.at[at], send_sem=sent, recv_sem=received,
                device_id={"seq": t}, device_id_type=MESH,
            ).start()

        @pl.loop(0, Z if k else Z - 1)
        def _(i):
            send(i)

    def wait_some(sem, ref, count):
        part = ref.at[pl.ds(0, count)]
        pltpu.make_async_copy(part, part, sem).wait()

    def wait_all(sem, ref):
        wait_some(sem, ref, SEQ - 1)

    def wait_group(sem, ref, k):
        @pl.when(k == 0)
        def _():
            wait_some(sem, ref, Z - 1)

        @pl.when(k > 0)
        def _():
            wait_some(sem, ref, Z)

    i = iota((G * C, G * C), 0)
    j = iota((G * C, G * C), 1)
    swap = one_hot(((i & (C - 1)) == (j >> 4)) & ((i >> 4) == (j & (G - 1))))

    cot_load.wait()

    @pl.loop(0, GROUPS)
    def _(g):
        rows = pl.ds(pl.multiple_of(g * G, G), G)
        cot_f[g] = mm(swap, cot_in[:, rows, :].reshape(C * G, N)).astype(BF16).reshape(G, C, N)

    pl.semaphore_wait(barrier, Q - 1 + Z - 1)

    @pl.loop(1, Z)
    def _(d):
        other = lax.rem(z + d, Z)
        pltpu.make_async_remote_copy(
            src_ref=cot_f.at[:, other], dst_ref=cot_z.at[z], send_sem=send_sem.at[0], recv_sem=recv_sem.at[0],
            device_id={"seq": q * Z + other}, device_id_type=MESH,
        ).start()

    for d in range(1, Z):
        pl.semaphore_signal(ready, inc=1, device_id={"seq": q * Z + lax.rem(z + d, Z)}, device_id_type=MESH)
    cot_z[z] = cot_f[:, z]

    clip_load.wait()
    sw_load.wait()
    tw_load.wait()
    for b in range(3):
        bands_s[b] = banded([sw_ref[a, b] for a in range(3)], G + 2, range(3), False)
        xs[b, 0] = jnp.zeros((C, N), BF16)
        xs[b, N + 1] = jnp.zeros((C, N), BF16)
    lane = iota((G * C, N), 1)

    @pl.loop(0, GROUPS)
    def _(g):
        rows = pl.ds(pl.multiple_of(g * G, G), G)
        x = mm(swap, clip_in[:, rows, :].reshape(C * G, N))
        padded = pl.ds(g * G + 1, G)
        xs[0, padded] = jnp.where(lane == 0, 0.0, pltpu.roll(x, 1, 1)).astype(BF16).reshape(G, C, N)
        xs[1, padded] = x.astype(BF16).reshape(G, C, N)
        xs[2, padded] = jnp.where(lane == N - 1, 0.0, pltpu.roll(x, N - 1, 1)).astype(BF16).reshape(G, C, N)

    @pl.loop(0, GROUPS)
    def _(g):
        p = jnp.zeros((G * C, N), F32)
        for b in range(3):
            p = p + mm(bands_s[b], xs[b, pl.ds(g * G, G + 2)].reshape((G + 2) * C, N))
        rows = pl.ds(g * G, G)
        preact[rows] = p.reshape(G, C, N)
        act_f[rows] = (p / (1.0 + jnp.exp(-p))).astype(BF16).reshape(G, C, N)

    pl.semaphore_wait(ready, Z - 1)

    def send_activated(k):
        if k >= 4:
            wait_some(send_act.at[k - 4], act_f, Z if k > 4 else Z - 1)
        send_group(k, act_f, st0, me + PAD, send_act.at[k], recv_sem.at[1])

    for k in range(4):
        send_activated(k)
    st0[me + PAD] = act_f[me]

    zeros = jnp.zeros((PAD, C, N), BF16)
    for ref in (back3, back2, back1, st0, st1, st2):
        ref[pl.ds(0, PAD)] = zeros
        ref[pl.ds(N + PAD, PAD)] = zeros
    for layer in range(3):
        e = 2**layer
        span = G + 2 * e
        taps = [tw_ref[layer, k] for k in range(3)]
        bands_b[layer, :, pl.ds(0, span * C)] = banded(taps, span, [(2 - k) * e for k in range(3)], True)
        bands_f[layer, :, pl.ds(0, span * C)] = banded(taps, span, [k * e for k in range(3)], False)

    def temporal(src, dst, bands, layer, pad):
        e = 2**layer
        span = G + 2 * e

        @pl.loop(0, GROUPS)
        def _(g):
            own = src[pl.ds(g * G + PAD, G)].reshape(G * C, N).astype(F32)
            wide = src[pl.ds(g * G + PAD - e, span)].reshape(span * C, N)
            new = own + mm(bands[layer, :, pl.ds(0, span * C)], wide)
            dst[pl.ds(g * G + pad, G)] = new.astype(BF16).reshape(G, C, N)

    wait_some(recv_sem.at[0], cot_z, Z - 1)
    own_frames = pl.ds(q * Z + PAD, Z)
    for k in range(1, Q):
        other = lax.rem(q + k, Q)
        pltpu.make_async_remote_copy(
            src_ref=cot_z.at[:, other], dst_ref=back3.at[own_frames], send_sem=send_sem.at[2], recv_sem=recv_sem.at[2],
            device_id={"seq": other * Z + z}, device_id_type=MESH,
        ).start()
    back3[own_frames] = cot_z[:, q]
    for k in range(4, Q):
        send_activated(k)

    wait_some(recv_sem.at[2], back3, SEQ - Z)
    temporal(back3, back2, bands_b, 2, PAD)
    temporal(back2, back1, bands_b, 1, PAD)
    temporal(back1, back0, bands_b, 0, 0)
    for k in range(Q):
        send_group(k, back0, grad_f, me, send_sem.at[1], recv_grad.at[k])
    grad_f[me] = back0[me]
    for b in range(3):
        bands_v[b] = banded([sw_ref[a, b] for a in range(3)], G + 2, [2 - a for a in range(3)], True, True)
        slopes[b, 0] = jnp.zeros((C, N), BF16)
        slopes[b, N + 1] = jnp.zeros((C, N), BF16)

    wait_all(recv_sem.at[1], st0)
    temporal(st0, st1, bands_f, 0, PAD)
    temporal(st1, st2, bands_f, 1, PAD)
    temporal(st2, st3, bands_f, 2, 0)

    def send_output(k):
        if k >= 3:
            wait_some(send_out.at[k - 3], st3, Z if k > 3 else Z - 1)
        send_group(k, st3, out_f, me, send_out.at[k], recv_out.at[k])

    for k in range(2):
        send_output(k)
    out_f[me] = st3[me]

    block = iota((C, 128), 1) >> 4
    last = jnp.zeros((C, 128), F32)
    packed = jnp.zeros((C, 128), F32)
    for layer, (state, back) in enumerate(((st0, back1), (st1, back2), (st2, back3))):
        e = 2**layer
        span = G + 2 * e
        acc_t[...] = jnp.zeros_like(acc_t)

        @pl.loop(0, GROUPS)
        def _(g):
            wide = state[pl.ds(g * G + PAD - e, span)].reshape(span * C, N)
            own = back[pl.ds(g * G + PAD, G)].reshape(G * C, N)
            acc_t[pl.ds(0, span * C)] += mm_nt(wide, own)

        for k in range(3):
            folded = fold(acc_t[pl.ds(0, span * C)], span, k * e)
            if layer * 3 + k < 8:
                packed = jnp.where(block == layer * 3 + k, folded, packed)
            else:
                last = jnp.where((block & 1) == 1, folded, last)
    packed_t = packed

    acc_s[...] = jnp.zeros_like(acc_s)

    @pl.loop(0, GROUPS)
    def _(k):
        wait_group(recv_grad.at[k], grad_f, k)
        g = lax.rem(q + Q - k, Q)
        rows = pl.ds(g * G, G)
        p = preact[rows].reshape(G * C, N)
        s = 1.0 / (1.0 + jnp.exp(-p))
        slope = grad_f[rows].reshape(G * C, N).astype(F32) * (s * (1.0 + p * (1.0 - s)))
        own = slope.astype(BF16)
        padded = pl.ds(g * G + 1, G)
        slopes[0, padded] = jnp.where(lane == N - 1, 0.0, pltpu.roll(slope, N - 1, 1)).astype(BF16).reshape(G, C, N)
        slopes[1, padded] = own.reshape(G, C, N)
        slopes[2, padded] = jnp.where(lane == 0, 0.0, pltpu.roll(slope, 1, 1)).astype(BF16).reshape(G, C, N)
        for b in range(3):
            acc_s[b] += mm_nt(xs[b, pl.ds(g * G, G + 2)].reshape((G + 2) * C, N), own)

    packed_s = jnp.zeros((C, 128), F32)
    for b in range(3):
        for a in range(3):
            folded = fold(acc_s[b], G + 2, a)
            if a * 3 + b < 8:
                packed_s = jnp.where(block == a * 3 + b, folded, packed_s)
            else:
                last = jnp.where((block & 1) == 0, folded, last)
    packed_l = jnp.zeros((4, 128), F32)
    for m in range(4):
        packed_l = jnp.where((block[:4] >> 1) == m, last[4 * m : 4 * m + 4], packed_l)
    for m in range(PIECES // 2):
        pack[m, :2] = packed_s[2 * m : 2 * m + 2]
        pack[m + 8, :2] = packed_t[2 * m : 2 * m + 2]
        pack[m, 2:] = packed_l[m : m + 1] if m < 4 else jnp.zeros((1, 128), F32)
        pack[m + 8, 2:] = jnp.zeros((1, 128), F32)

    piece = q * 2 + lax.rem(z, 2)
    pair = z // 2

    def to_group(src_of, dst, index):
        @pl.loop(1, PIECES)
        def _(d):
            other = lax.rem(piece + d, PIECES)
            pltpu.make_async_remote_copy(
                src_ref=src_of(other), dst_ref=dst.at[piece], send_sem=send_sem.at[index], recv_sem=recv_sem.at[index],
                device_id={"seq": (other // 2) * Z + pair * 2 + lax.rem(other, 2)}, device_id_type=MESH,
            ).start()

    def clip_gradient(g):
        total = jnp.zeros((C * G, N), F32)
        for b in range(3):
            total = total + mm(bands_v[b], slopes[b, pl.ds(g * G, G + 2)].reshape((G + 2) * C, N))
        grad_v[:, pl.ds(pl.multiple_of(g * G, G), G), :] = total.astype(BF16).reshape(C, G, N)

    to_group(lambda other: pack.at[other], sum1, 3)
    sum1[piece] = pack[piece]
    send_output(2)
    send_output(3)

    @pl.loop(0, GROUPS // 2)
    def _(g):
        clip_gradient(g)

    wait_some(recv_sem.at[3], sum1, PIECES - 1)
    part1[...] = jnp.sum(sum1[...], axis=0)
    for d in range(1, Z // 2):
        other = lax.rem(z + 2 * d, Z)
        pltpu.make_async_remote_copy(
            src_ref=part1, dst_ref=sum2.at[pair], send_sem=send_sem.at[4], recv_sem=recv_sem.at[4],
            device_id={"seq": q * Z + other}, device_id_type=MESH,
        ).start()
    sum2[pair] = part1[...]
    send_output(4)
    send_output(5)

    @pl.loop(GROUPS // 2, GROUPS)
    def _(g):
        clip_gradient(g)

    grad_store = pltpu.make_async_copy(grad_v, grad_hbm.at[0], local_sem.at[0])
    grad_store.start()
    send_output(6)
    send_output(7)

    wait_some(recv_sem.at[4], sum2, Z // 2 - 1)
    part2[...] = jnp.sum(sum2[...], axis=0)
    to_group(lambda other: part2, sum3, 5)
    sum3[piece] = part2[...]

    def output_rows(k):
        wait_group(recv_out.at[k], out_f, k)
        rows = pl.ds(pl.multiple_of(lax.rem(q + Q - k, Q) * G, G), G)
        out_v[:, rows, :] = mm(swap, out_f[rows].reshape(G * C, N)).astype(BF16).reshape(C, G, N)
        pltpu.make_async_copy(out_v.at[:, rows, :], out_hbm.at[0, :, rows, :], local_sem.at[1]).start()

    @pl.loop(0, GROUPS - 1)
    def _(k):
        output_rows(k)

    wait_some(recv_sem.at[5], sum3, PIECES - 1)
    for m in range(PIECES):
        total[pl.ds(2 * m, 2)] = sum3[m, :2] * factor
    for m in range(4):
        total[pl.ds(32 + m, 1)] = sum3[m, 2:] * factor
    last = total[pl.ds(32, 4)]
    for tap in range(9):
        at = (128 - tap * C) % 128
        if tap < 8:
            sgrad_ref[tap // 3, tap % 3] = pltpu.roll(total[pl.ds(0, C)], at, 1)[:, :C] if at else total[pl.ds(0, C)][:, :C]
            tgrad_ref[tap // 3, tap % 3] = pltpu.roll(total[pl.ds(C, C)], at, 1)[:, :C] if at else total[pl.ds(C, C)][:, :C]
        else:
            for m in range(4):
                back_by = (128 - 32 * m) % 128
                sgrad_ref[2, 2, pl.ds(4 * m, 4)] = (pltpu.roll(last, back_by, 1) if back_by else last)[:, :C]
                tgrad_ref[2, 2, pl.ds(4 * m, 4)] = pltpu.roll(last, back_by - C if m else 128 - C, 1)[:, :C]

    small_stores = [
        pltpu.make_async_copy(sgrad_ref, sgrad_hbm, local_sem.at[2]),
        pltpu.make_async_copy(tgrad_ref, tgrad_hbm, local_sem.at[3]),
    ]
    for store in small_stores:
        store.start()

    output_rows(GROUPS - 1)

    wait_some(send_sem.at[0], cot_z, Z - 1)
    wait_all(send_sem.at[1], back0)
    wait_some(send_sem.at[2], back3, SEQ - Z)
    for k in range(4, Q):
        wait_some(send_act.at[k], act_f, Z)
    for k in range(5, Q):
        wait_some(send_out.at[k], st3, Z)
    wait_some(send_sem.at[3], sum1, PIECES - 1)
    wait_some(send_sem.at[4], sum2, Z // 2 - 1)
    wait_some(send_sem.at[5], sum3, PIECES - 1)
    for store in small_stores:
        store.wait()
    grad_store.wait()
    pltpu.make_async_copy(out_v, out_hbm.at[0], local_sem.at[1]).wait()


def hand_over(out_in, grad_in, sgrad_in, tgrad_in, out_hbm, grad_hbm, sgrad_hbm, tgrad_hbm, *scratch):
    stages, load_sem, store_sem = scratch[:4], scratch[4], scratch[5]
    loads, stores = [], []
    pairs = zip((out_in, grad_in, sgrad_in, tgrad_in), stages, (out_hbm, grad_hbm, sgrad_hbm, tgrad_hbm))
    for source, stage, target in pairs:
        for part in range(HANDED if source.shape[0] == 1 else 1):
            at = (0, pl.ds(part * C // HANDED, C // HANDED)) if source.shape[0] == 1 else slice(None)
            loads.append(pltpu.make_async_copy(source.at[at], stage.at[at], load_sem.at[len(loads)]))
            stores.append(pltpu.make_async_copy(stage.at[at], target.at[at], store_sem.at[len(stores)]))
    for load in loads:
        load.start()
    for load, store in zip(loads, stores):
        load.wait()
        store.start()
    for store in stores:
        store.wait()


def body(clip_frames, cotangent, spatial_weight, temporal_weight):
    factor = 1.0 / math.sqrt(N * N * N)
    anywhere = pl.BlockSpec(memory_space=pltpu.HBM)
    frame = pltpu.VMEM((N, C, N), BF16)
    padded = pltpu.VMEM((N + 2 * PAD, C, N), BF16)
    results = pl.pallas_call(
        functools.partial(kernel, factor),
        out_shape=(
            jax.ShapeDtypeStruct((1, C, N, N), BF16),
            jax.ShapeDtypeStruct((1, C, N, N), BF16),
            jax.ShapeDtypeStruct((3, 3, C, C), F32),
            jax.ShapeDtypeStruct((3, 3, C, C), F32),
        ),
        in_specs=[anywhere] * 4,
        out_specs=(anywhere,) * 4,
        scratch_shapes=[
            pltpu.VMEM((3, 3, C, C), BF16),
            pltpu.VMEM((3, 3, C, C), BF16),
            pltpu.VMEM((3, 3, C, C), F32),
            pltpu.VMEM((3, 3, C, C), F32),
            pltpu.VMEM((C, N, N), BF16),
            pltpu.VMEM((C, N, N), BF16),
            pltpu.VMEM((Q, Z, C, N), BF16),
            pltpu.VMEM((Z, Q, C, N), BF16),
            frame,
            pltpu.VMEM((3, N + 2, C, N), BF16),
            pltpu.VMEM((N, C, N), F32),
            pltpu.VMEM((3, G * C, (G + 2) * C), BF16),
            pltpu.VMEM((3, G * C, (G + 2) * C), BF16),
            pltpu.VMEM((3, G * C, (G + 8) * C), BF16),
            pltpu.VMEM((3, G * C, (G + 8) * C), BF16),
            padded, padded, padded, frame,
            padded, padded, padded, frame,
            frame,
            frame,
            pltpu.VMEM((3, N + 2, C, N), BF16),
            pltpu.VMEM(((G + 8) * C, G * C), F32),
            pltpu.VMEM((3, (G + 2) * C, G * C), F32),
            pltpu.VMEM((PIECES, PIECE, 128), F32),
            pltpu.VMEM((PIECES, PIECE, 128), F32),
            pltpu.VMEM((PIECE, 128), F32),
            pltpu.VMEM((Z // 2, PIECE, 128), F32),
            pltpu.VMEM((PIECE, 128), F32),
            pltpu.VMEM((PIECES, PIECE, 128), F32),
            pltpu.VMEM((40, 128), F32),
            pltpu.VMEM((C, N, N), BF16),
            pltpu.VMEM((C, N, N), BF16),
            pltpu.SemaphoreType.DMA((4,)),
            pltpu.SemaphoreType.DMA((6,)),
            pltpu.SemaphoreType.DMA((6,)),
            pltpu.SemaphoreType.DMA((Q,)),
            pltpu.SemaphoreType.DMA((Q,)),
            pltpu.SemaphoreType.DMA((Q,)),
            pltpu.SemaphoreType.DMA((Q,)),
            pltpu.SemaphoreType.REGULAR,
        ],
        compiler_params=pltpu.CompilerParams(collective_id=0, has_side_effects=True, vmem_limit_bytes=VMEM_LIMIT),
    )(clip_frames, cotangent, spatial_weight, temporal_weight)
    return pl.pallas_call(
        hand_over,
        out_shape=tuple(jax.ShapeDtypeStruct(r.shape, r.dtype) for r in results),
        in_specs=[anywhere] * 4,
        out_specs=(anywhere,) * 4,
        scratch_shapes=[pltpu.VMEM(r.shape, r.dtype) for r in results] + [pltpu.SemaphoreType.DMA((2 * HANDED + 2,))] * 2,
        compiler_params=pltpu.CompilerParams(vmem_limit_bytes=VMEM_LIMIT),
    )(*results)


def solution(mesh):
    placed = (P(("dp", "seq"), None, None, None), P(("dp", "seq"), None, None, None), P(), P())
    return jax.shard_map(
        body,
        mesh=mesh,
        in_specs=placed,
        out_specs=(
            P(("dp", "seq"), None, None, None),
            P(("dp", "seq"), None, None, None),
            P("dp", None, None, None),
            P("dp", None, None, None),
        ),
        check_vma=False,
    )
```

```python
import functools
import math

import jax
import jax.numpy as jnp
from jax import lax
from jax.experimental import pallas as pl
from jax.experimental.pallas import tpu as pltpu
from jax.sharding import PartitionSpec as P

MESH = pl.DeviceIdType.MESH
F32 = jnp.float32
BF16 = jnp.bfloat16
C = 16
N = 128
SEQ = 128
Z = 16
Q = SEQ // Z
G = 16
GROUPS = N // G
PAD = 4
PIECES = 2 * Q
PIECE = 3
VMEM_LIMIT = 60 << 20
HANDED = 1


def iota(shape, axis):
    return lax.broadcasted_iota(jnp.int32, shape, axis)


def mm(a, b):
    return lax.dot_general(a, b, (((1,), (0,)), ((), ())), preferred_element_type=F32)


def mm_nt(a, b):
    return lax.dot_general(a, b, (((1,), (1,)), ((), ())), preferred_element_type=F32)


def one_hot(cond):
    return jnp.where(cond, 1.0, 0.0).astype(BF16)


def banded(weights, span, offsets, transposed, out_channel_major=False):
    cols = span * C
    i = iota((G * C, cols), 0)
    j = iota((G * C, cols), 1)
    si = iota((G * C, C), 0)
    sj = iota((G * C, C), 1)
    if out_channel_major:
        place = i & (G - 1)
        spread = one_hot((si >> 4) == sj)
    else:
        place = i >> 4
        spread = one_hot((si & (C - 1)) == sj)
    tile = one_hot(iota((C, cols), 0) == (iota((C, cols), 1) & (C - 1)))
    diff = (j >> 4) - place
    total = jnp.zeros((G * C, cols), F32)
    for weight, offset in zip(weights, offsets):
        rows = (mm if transposed else mm_nt)(spread, weight).astype(BF16)
        total = jnp.where(diff == offset, mm(rows, tile), total)
    return total.astype(BF16)


def fold(acc, span, offset):
    rows = span * C
    diff = (iota((rows, G * C), 0) >> 4) - (iota((rows, G * C), 1) >> 4)
    kept = jnp.where(diff == offset, acc, 0.0)
    total = jnp.sum(kept.reshape(span, C, G * C), axis=0)
    total = total[:, :128] + total[:, 128:]
    for step in (64, 32, 16):
        total = total + pltpu.roll(total, step, 1)
    return total


def kernel(
    factor,
    clip_hbm, cot_hbm, sw_hbm, tw_hbm,
    out_hbm, grad_hbm, sgrad_hbm, tgrad_hbm,
    sw_ref, tw_ref, sgrad_ref, tgrad_ref, clip_in, cot_in, cot_f, cot_z, act_f, xs, preact, bands_s, bands_v, bands_f, bands_b,
    back3, back2, back1, back0, st0, st1, st2, st3, grad_f, out_f, slopes,
    acc_t, acc_s, pack, sum1, part1, sum2, part2, sum3, total, out_v, grad_v,
    local_sem, send_sem, recv_sem, send_act, send_out, recv_grad, recv_out, ready,
):
    me = lax.axis_index("seq")
    q, z = me // Z, lax.rem(me, Z)

    far_first = sorted(range(1, Z), key=lambda d: -min(d, Z - d))
    barrier = pltpu.get_barrier_semaphore()
    for d in far_first:
        pl.semaphore_signal(barrier, inc=1, device_id={"seq": q * Z + lax.rem(z + d, Z)}, device_id_type=MESH)
    for d in range(1, Q):
        pl.semaphore_signal(barrier, inc=1, device_id={"seq": lax.rem(q + d, Q) * Z + z}, device_id_type=MESH)

    cot_load = pltpu.make_async_copy(cot_hbm.at[0], cot_in, local_sem.at[0])
    cot_load.start()
    clip_load = pltpu.make_async_copy(clip_hbm.at[0], clip_in, local_sem.at[1])
    clip_load.start()
    sw_load = pltpu.make_async_copy(sw_hbm, sw_ref, local_sem.at[2])
    sw_load.start()
    tw_load = pltpu.make_async_copy(tw_hbm, tw_ref, local_sem.at[3])
    tw_load.start()

    def send_group(k, src, dst, at, sent, received):
        column = lax.rem(q + k, Q) * Z

        def send(i):
            j = 8 + lax.rem(i, 2) * (i + 1) // 2 - (1 - lax.rem(i, 2)) * (i // 2)
            t = column + lax.rem(z + j, Z)
            pltpu.make_async_remote_copy(
                src_ref=src.at[t], dst_ref=dst.at[at], send_sem=sent, recv_sem=received,
                device_id={"seq": t}, device_id_type=MESH,
            ).start()

        @pl.loop(0, Z if k else Z - 1)
        def _(i):
            send(i)

    def wait_some(sem, ref, count):
        part = ref.at[pl.ds(0, count)]
        pltpu.make_async_copy(part, part, sem).wait()

    def wait_all(sem, ref):
        wait_some(sem, ref, SEQ - 1)

    def wait_group(sem, ref, k):
        @pl.when(k == 0)
        def _():
            wait_some(sem, ref, Z - 1)

        @pl.when(k > 0)
        def _():
            wait_some(sem, ref, Z)

    i = iota((G * C, G * C), 0)
    j = iota((G * C, G * C), 1)
    swap = one_hot(((i & (C - 1)) == (j >> 4)) & ((i >> 4) == (j & (G - 1))))

    cot_load.wait()

    @pl.loop(0, GROUPS)
    def _(g):
        rows = pl.ds(pl.multiple_of(g * G, G), G)
        cot_f[g] = mm(swap, cot_in[:, rows, :].reshape(C * G, N)).astype(BF16).reshape(G, C, N)

    pl.semaphore_wait(barrier, Q - 1 + Z - 1)

    for d in far_first:
        other = lax.rem(z + d, Z)
        pltpu.make_async_remote_copy(
            src_ref=cot_f.at[:, other], dst_ref=cot_z.at[z], send_sem=send_sem.at[0], recv_sem=recv_sem.at[0],
            device_id={"seq": q * Z + other}, device_id_type=MESH,
        ).start()

    for d in range(1, Z):
        pl.semaphore_signal(ready, inc=1, device_id={"seq": q * Z + lax.rem(z + d, Z)}, device_id_type=MESH)
    cot_z[z] = cot_f[:, z]

    clip_load.wait()
    sw_load.wait()
    tw_load.wait()
    for b in range(3):
        bands_s[b] = banded([sw_ref[a, b] for a in range(3)], G + 2, range(3), False)
        xs[b, 0] = jnp.zeros((C, N), BF16)
        xs[b, N + 1] = jnp.zeros((C, N), BF16)
    lane = iota((G * C, N), 1)

    @pl.loop(0, GROUPS)
    def _(g):
        rows = pl.ds(pl.multiple_of(g * G, G), G)
        x = mm(swap, clip_in[:, rows, :].reshape(C * G, N))
        padded = pl.ds(g * G + 1, G)
        xs[0, padded] = jnp.where(lane == 0, 0.0, pltpu.roll(x, 1, 1)).astype(BF16).reshape(G, C, N)
        xs[1, padded] = x.astype(BF16).reshape(G, C, N)
        xs[2, padded] = jnp.where(lane == N - 1, 0.0, pltpu.roll(x, N - 1, 1)).astype(BF16).reshape(G, C, N)

    @pl.loop(0, GROUPS)
    def _(g):
        p = jnp.zeros((G * C, N), F32)
        for b in range(3):
            p = p + mm(bands_s[b], xs[b, pl.ds(g * G, G + 2)].reshape((G + 2) * C, N))
        rows = pl.ds(g * G, G)
        preact[rows] = p.reshape(G, C, N)
        act_f[rows] = (p / (1.0 + jnp.exp(-p))).astype(BF16).reshape(G, C, N)

    pl.semaphore_wait(ready, Z - 1)

    def send_activated(k):
        if k >= 4:
            wait_some(send_act.at[k - 4], act_f, Z if k > 4 else Z - 1)
        send_group(k, act_f, st0, me + PAD, send_act.at[k], recv_sem.at[1])

    for k in range(4):
        send_activated(k)
    st0[me + PAD] = act_f[me]

    zeros = jnp.zeros((PAD, C, N), BF16)
    for ref in (back3, back2, back1, st0, st1, st2):
        ref[pl.ds(0, PAD)] = zeros
        ref[pl.ds(N + PAD, PAD)] = zeros
    for layer in range(3):
        e = 2**layer
        span = G + 2 * e
        taps = [tw_ref[layer, k] for k in range(3)]
        bands_b[layer, :, pl.ds(0, span * C)] = banded(taps, span, [(2 - k) * e for k in range(3)], True)
        bands_f[layer, :, pl.ds(0, span * C)] = banded(taps, span, [k * e for k in range(3)], False)

    def temporal(src, dst, bands, layer, pad):
        e = 2**layer
        span = G + 2 * e

        @pl.loop(0, GROUPS)
        def _(g):
            own = src[pl.ds(g * G + PAD, G)].reshape(G * C, N).astype(F32)
            wide = src[pl.ds(g * G + PAD - e, span)].reshape(span * C, N)
            new = own + mm(bands[layer, :, pl.ds(0, span * C)], wide)
            dst[pl.ds(g * G + pad, G)] = new.astype(BF16).reshape(G, C, N)

    wait_some(recv_sem.at[0], cot_z, Z - 1)
    own_frames = pl.ds(q * Z + PAD, Z)
    for k in range(1, Q):
        other = lax.rem(q + k, Q)
        pltpu.make_async_remote_copy(
            src_ref=cot_z.at[:, other], dst_ref=back3.at[own_frames], send_sem=send_sem.at[2], recv_sem=recv_sem.at[2],
            device_id={"seq": other * Z + z}, device_id_type=MESH,
        ).start()
    back3[own_frames] = cot_z[:, q]
    for k in range(4, Q):
        send_activated(k)

    wait_some(recv_sem.at[2], back3, SEQ - Z)
    temporal(back3, back2, bands_b, 2, PAD)
    temporal(back2, back1, bands_b, 1, PAD)
    temporal(back1, back0, bands_b, 0, 0)
    for k in range(Q):
        send_group(k, back0, grad_f, me, send_sem.at[1], recv_grad.at[k])
    grad_f[me] = back0[me]
    for b in range(3):
        bands_v[b] = banded([sw_ref[a, b] for a in range(3)], G + 2, [2 - a for a in range(3)], True, True)
        slopes[b, 0] = jnp.zeros((C, N), BF16)
        slopes[b, N + 1] = jnp.zeros((C, N), BF16)

    wait_all(recv_sem.at[1], st0)
    temporal(st0, st1, bands_f, 0, PAD)
    temporal(st1, st2, bands_f, 1, PAD)
    temporal(st2, st3, bands_f, 2, 0)

    def send_output(k):
        if k >= 3:
            wait_some(send_out.at[k - 3], st3, Z if k > 3 else Z - 1)
        send_group(k, st3, out_f, me, send_out.at[k], recv_out.at[k])

    for k in range(2):
        send_output(k)
    out_f[me] = st3[me]

    block = iota((C, 128), 1) >> 4
    last = jnp.zeros((C, 128), F32)
    packed = jnp.zeros((C, 128), F32)
    for layer, (state, back) in enumerate(((st0, back1), (st1, back2), (st2, back3))):
        e = 2**layer
        span = G + 2 * e
        acc_t[...] = jnp.zeros_like(acc_t)

        @pl.loop(0, GROUPS)
        def _(g):
            wide = state[pl.ds(g * G + PAD - e, span)].reshape(span * C, N)
            own = back[pl.ds(g * G + PAD, G)].reshape(G * C, N)
            acc_t[pl.ds(0, span * C)] += mm_nt(wide, own)

        for k in range(3):
            folded = fold(acc_t[pl.ds(0, span * C)], span, k * e)
            if layer * 3 + k < 8:
                packed = jnp.where(block == layer * 3 + k, folded, packed)
            else:
                last = jnp.where((block & 1) == 1, folded, last)
    packed_t = packed

    acc_s[...] = jnp.zeros_like(acc_s)

    @pl.loop(0, GROUPS)
    def _(k):
        wait_group(recv_grad.at[k], grad_f, k)
        g = lax.rem(q + Q - k, Q)
        rows = pl.ds(g * G, G)
        p = preact[rows].reshape(G * C, N)
        s = 1.0 / (1.0 + jnp.exp(-p))
        slope = grad_f[rows].reshape(G * C, N).astype(F32) * (s * (1.0 + p * (1.0 - s)))
        own = slope.astype(BF16)
        padded = pl.ds(g * G + 1, G)
        slopes[0, padded] = jnp.where(lane == N - 1, 0.0, pltpu.roll(slope, N - 1, 1)).astype(BF16).reshape(G, C, N)
        slopes[1, padded] = own.reshape(G, C, N)
        slopes[2, padded] = jnp.where(lane == 0, 0.0, pltpu.roll(slope, 1, 1)).astype(BF16).reshape(G, C, N)
        for b in range(3):
            acc_s[b] += mm_nt(xs[b, pl.ds(g * G, G + 2)].reshape((G + 2) * C, N), own)

    packed_s = jnp.zeros((C, 128), F32)
    for b in range(3):
        for a in range(3):
            folded = fold(acc_s[b], G + 2, a)
            if a * 3 + b < 8:
                packed_s = jnp.where(block == a * 3 + b, folded, packed_s)
            else:
                last = jnp.where((block & 1) == 0, folded, last)
    packed_l = jnp.zeros((4, 128), F32)
    for m in range(4):
        packed_l = jnp.where((block[:4] >> 1) == m, last[4 * m : 4 * m + 4], packed_l)
    for m in range(PIECES // 2):
        pack[m, :2] = packed_s[2 * m : 2 * m + 2]
        pack[m + 8, :2] = packed_t[2 * m : 2 * m + 2]
        pack[m, 2:] = packed_l[m : m + 1] if m < 4 else jnp.zeros((1, 128), F32)
        pack[m + 8, 2:] = jnp.zeros((1, 128), F32)

    piece = q * 2 + lax.rem(z, 2)
    pair = z // 2

    def to_group(src_of, dst, index):
        @pl.loop(1, PIECES)
        def _(d):
            other = lax.rem(piece + d, PIECES)
            pltpu.make_async_remote_copy(
                src_ref=src_of(other), dst_ref=dst.at[piece], send_sem=send_sem.at[index], recv_sem=recv_sem.at[index],
                device_id={"seq": (other // 2) * Z + pair * 2 + lax.rem(other, 2)}, device_id_type=MESH,
            ).start()

    def clip_gradient(g):
        total = jnp.zeros((C * G, N), F32)
        for b in range(3):
            total = total + mm(bands_v[b], slopes[b, pl.ds(g * G, G + 2)].reshape((G + 2) * C, N))
        grad_v[:, pl.ds(pl.multiple_of(g * G, G), G), :] = total.astype(BF16).reshape(C, G, N)

    to_group(lambda other: pack.at[other], sum1, 3)
    sum1[piece] = pack[piece]
    send_output(2)
    send_output(3)

    @pl.loop(0, GROUPS // 2)
    def _(g):
        clip_gradient(g)

    wait_some(recv_sem.at[3], sum1, PIECES - 1)
    part1[...] = jnp.sum(sum1[...], axis=0)
    for d in range(1, Z // 2):
        other = lax.rem(z + 2 * d, Z)
        pltpu.make_async_remote_copy(
            src_ref=part1, dst_ref=sum2.at[pair], send_sem=send_sem.at[4], recv_sem=recv_sem.at[4],
            device_id={"seq": q * Z + other}, device_id_type=MESH,
        ).start()
    sum2[pair] = part1[...]
    send_output(4)
    send_output(5)

    @pl.loop(GROUPS // 2, GROUPS)
    def _(g):
        clip_gradient(g)

    grad_store = pltpu.make_async_copy(grad_v, grad_hbm.at[0], local_sem.at[0])
    grad_store.start()
    send_output(6)
    send_output(7)

    wait_some(recv_sem.at[4], sum2, Z // 2 - 1)
    part2[...] = jnp.sum(sum2[...], axis=0)
    to_group(lambda other: part2, sum3, 5)
    sum3[piece] = part2[...]

    def output_rows(k):
        wait_group(recv_out.at[k], out_f, k)
        rows = pl.ds(pl.multiple_of(lax.rem(q + Q - k, Q) * G, G), G)
        out_v[:, rows, :] = mm(swap, out_f[rows].reshape(G * C, N)).astype(BF16).reshape(C, G, N)
        pltpu.make_async_copy(out_v.at[:, rows, :], out_hbm.at[0, :, rows, :], local_sem.at[1]).start()

    @pl.loop(0, GROUPS - 1)
    def _(k):
        output_rows(k)

    wait_some(recv_sem.at[5], sum3, PIECES - 1)
    for m in range(PIECES):
        total[pl.ds(2 * m, 2)] = sum3[m, :2] * factor
    for m in range(4):
        total[pl.ds(32 + m, 1)] = sum3[m, 2:] * factor
    last = total[pl.ds(32, 4)]
    for tap in range(9):
        at = (128 - tap * C) % 128
        if tap < 8:
            sgrad_ref[tap // 3, tap % 3] = pltpu.roll(total[pl.ds(0, C)], at, 1)[:, :C] if at else total[pl.ds(0, C)][:, :C]
            tgrad_ref[tap // 3, tap % 3] = pltpu.roll(total[pl.ds(C, C)], at, 1)[:, :C] if at else total[pl.ds(C, C)][:, :C]
        else:
            for m in range(4):
                back_by = (128 - 32 * m) % 128
                sgrad_ref[2, 2, pl.ds(4 * m, 4)] = (pltpu.roll(last, back_by, 1) if back_by else last)[:, :C]
                tgrad_ref[2, 2, pl.ds(4 * m, 4)] = pltpu.roll(last, back_by - C if m else 128 - C, 1)[:, :C]

    small_stores = [
        pltpu.make_async_copy(sgrad_ref, sgrad_hbm, local_sem.at[2]),
        pltpu.make_async_copy(tgrad_ref, tgrad_hbm, local_sem.at[3]),
    ]
    for store in small_stores:
        store.start()

    output_rows(GROUPS - 1)

    wait_some(send_sem.at[0], cot_z, Z - 1)
    wait_all(send_sem.at[1], back0)
    wait_some(send_sem.at[2], back3, SEQ - Z)
    for k in range(4, Q):
        wait_some(send_act.at[k], act_f, Z)
    for k in range(5, Q):
        wait_some(send_out.at[k], st3, Z)
    wait_some(send_sem.at[3], sum1, PIECES - 1)
    wait_some(send_sem.at[4], sum2, Z // 2 - 1)
    wait_some(send_sem.at[5], sum3, PIECES - 1)
    for store in small_stores:
        store.wait()
    grad_store.wait()
    pltpu.make_async_copy(out_v, out_hbm.at[0], local_sem.at[1]).wait()


def hand_over(out_in, grad_in, sgrad_in, tgrad_in, out_hbm, grad_hbm, sgrad_hbm, tgrad_hbm, *scratch):
    stages, load_sem, store_sem = scratch[:4], scratch[4], scratch[5]
    loads, stores = [], []
    pairs = zip((out_in, grad_in, sgrad_in, tgrad_in), stages, (out_hbm, grad_hbm, sgrad_hbm, tgrad_hbm))
    for source, stage, target in pairs:
        for part in range(HANDED if source.shape[0] == 1 else 1):
            at = (0, pl.ds(part * C // HANDED, C // HANDED)) if source.shape[0] == 1 else slice(None)
            loads.append(pltpu.make_async_copy(source.at[at], stage.at[at], load_sem.at[len(loads)]))
            stores.append(pltpu.make_async_copy(stage.at[at], target.at[at], store_sem.at[len(stores)]))
    for load in loads:
        load.start()
    for load, store in zip(loads, stores):
        load.wait()
        store.start()
    for store in stores:
        store.wait()


def body(clip_frames, cotangent, spatial_weight, temporal_weight):
    factor = 1.0 / math.sqrt(N * N * N)
    anywhere = pl.BlockSpec(memory_space=pltpu.HBM)
    frame = pltpu.VMEM((N, C, N), BF16)
    padded = pltpu.VMEM((N + 2 * PAD, C, N), BF16)
    results = pl.pallas_call(
        functools.partial(kernel, factor),
        out_shape=(
            jax.ShapeDtypeStruct((1, C, N, N), BF16),
            jax.ShapeDtypeStruct((1, C, N, N), BF16),
            jax.ShapeDtypeStruct((3, 3, C, C), F32),
            jax.ShapeDtypeStruct((3, 3, C, C), F32),
        ),
        in_specs=[anywhere] * 4,
        out_specs=(anywhere,) * 4,
        scratch_shapes=[
            pltpu.VMEM((3, 3, C, C), BF16),
            pltpu.VMEM((3, 3, C, C), BF16),
            pltpu.VMEM((3, 3, C, C), F32),
            pltpu.VMEM((3, 3, C, C), F32),
            pltpu.VMEM((C, N, N), BF16),
            pltpu.VMEM((C, N, N), BF16),
            pltpu.VMEM((Q, Z, C, N), BF16),
            pltpu.VMEM((Z, Q, C, N), BF16),
            frame,
            pltpu.VMEM((3, N + 2, C, N), BF16),
            pltpu.VMEM((N, C, N), F32),
            pltpu.VMEM((3, G * C, (G + 2) * C), BF16),
            pltpu.VMEM((3, G * C, (G + 2) * C), BF16),
            pltpu.VMEM((3, G * C, (G + 8) * C), BF16),
            pltpu.VMEM((3, G * C, (G + 8) * C), BF16),
            padded, padded, padded, frame,
            padded, padded, padded, frame,
            frame,
            frame,
            pltpu.VMEM((3, N + 2, C, N), BF16),
            pltpu.VMEM(((G + 8) * C, G * C), F32),
            pltpu.VMEM((3, (G + 2) * C, G * C), F32),
            pltpu.VMEM((PIECES, PIECE, 128), F32),
            pltpu.VMEM((PIECES, PIECE, 128), F32),
            pltpu.VMEM((PIECE, 128), F32),
            pltpu.VMEM((Z // 2, PIECE, 128), F32),
            pltpu.VMEM((PIECE, 128), F32),
            pltpu.VMEM((PIECES, PIECE, 128), F32),
            pltpu.VMEM((40, 128), F32),
            pltpu.VMEM((C, N, N), BF16),
            pltpu.VMEM((C, N, N), BF16),
            pltpu.SemaphoreType.DMA((4,)),
            pltpu.SemaphoreType.DMA((6,)),
            pltpu.SemaphoreType.DMA((6,)),
            pltpu.SemaphoreType.DMA((Q,)),
            pltpu.SemaphoreType.DMA((Q,)),
            pltpu.SemaphoreType.DMA((Q,)),
            pltpu.SemaphoreType.DMA((Q,)),
            pltpu.SemaphoreType.REGULAR,
        ],
        compiler_params=pltpu.CompilerParams(collective_id=0, has_side_effects=True, vmem_limit_bytes=VMEM_LIMIT),
    )(clip_frames, cotangent, spatial_weight, temporal_weight)
    return pl.pallas_call(
        hand_over,
        out_shape=tuple(jax.ShapeDtypeStruct(r.shape, r.dtype) for r in results),
        in_specs=[anywhere] * 4,
        out_specs=(anywhere,) * 4,
        scratch_shapes=[pltpu.VMEM(r.shape, r.dtype) for r in results] + [pltpu.SemaphoreType.DMA((2 * HANDED + 2,))] * 2,
        compiler_params=pltpu.CompilerParams(vmem_limit_bytes=VMEM_LIMIT),
    )(*results)


def solution(mesh):
    placed = (P(("dp", "seq"), None, None, None), P(("dp", "seq"), None, None, None), P(), P())
    return jax.shard_map(
        body,
        mesh=mesh,
        in_specs=placed,
        out_specs=(
            P(("dp", "seq"), None, None, None),
            P(("dp", "seq"), None, None, None),
            P("dp", None, None, None),
            P("dp", None, None, None),
        ),
        check_vma=False,
    )
```
